768 devices in a mesh: comp: 2 (over core), blk: 48 (over z, x), sub: 8 (over y).
Axes of the slice: x: 4, y: 8, z: 12, core: 2. Of those that a mesh axis runs over, the one named last changes fastest.
Arguments:
- ocean_state: float32 [3, 256, 12288], P(None, ('comp', 'sub'), 'blk'), may hold values from -4 to 4
- sea_temp: float32 [256, 12288], P(('comp', 'sub'), 'blk'), may hold values from -6 to 6
- land_mask: int32 [256, 12288], P(('comp', 'sub'), 'blk'), may hold values from 0 to 1, as said below
- atm_flux: bfloat16 [16, 3072, 12, 128], P(('comp', 'sub'), 'blk'), may hold values from -6 to 6
- remap_w: bfloat16 [256, 96, 3, 128, 128], P(('comp', 'sub'), 'blk'), may hold values from -0.3125 to 0.3125
- source_tile: int32 [256, 96, 3], P(('comp', 'sub'), 'blk'), may hold values from 0 to 3071, as said below
- send_tiles: int32 [16, 48, 48, 3], P(('comp', 'sub'), 'blk'), may hold values from -1 to 63, as said below
- flux_mix: float32 [3, 12], replicated, may hold values from -1.75 to 1.75
Outputs:
- ocean_out: float32 [3, 256, 12288], P(None, ('comp', 'sub'), 'blk')
- atm_surface: float32 [16, 3072, 2, 128], P(('comp', 'sub'), 'blk')
The draws below stay inside these ranges and needn't reach their ends.
Inputs may be any that keep to these rules, and one draw needn't show every extreme that they name: `source_tile`: each entry names a tile of the ocean tile's own band; value // 64 is the index along blk of the device that holds it. send_tiles[b, j, k] lists, in ascending order, the distinct tiles value % 64 of the source_tile entries of ocean block k of band b with value // 64 = j, followed by -1; every band has, for each j, some k, and for each k, some j, with all 3 filled. `land_mask`: the first and last rows of the grid are land.
All inputs are finite; a program needn't handle non-finite values.
Results may differ from the reference program's by a relative error of at most 0.0025.
Values may be sent and summed in bfloat16 or wider, within the bound.
A program may use at most 64 MiB of HBM per device.

```python
import jax
import jax.numpy as jnp
from jax import lax

FIELDS = 12
FORCINGS = 3
TILE = 128
KSRC = 3
CAP = 3
SUBCYCLES = 10
OY = 16
OX = 256
ATILES_DEV = 64
BANDS = 16
ATILES = 3072
NY = 256
NX = 12288
XTILES = 96
N_BLK = 48


def routing(key):
    refs_dev = KSRC * OY * OX // TILE
    band_keys = jax.random.split(key, BANDS)

    def one_band(band_key):
        key_dev, key_perm, key_tiles = jax.random.split(band_key, 3)
        chosen = jax.random.randint(key_dev, (N_BLK, refs_dev), 0, N_BLK)
        partner = jax.random.permutation(key_perm, N_BLK)
        column = jnp.arange(refs_dev)[None, :]
        chosen = jnp.where(column < CAP, partner[:, None], chosen).astype(jnp.int32)
        same_dev = chosen[:, :, None] == chosen[:, None, :]
        before = jnp.arange(refs_dev)[None, None, :] < jnp.arange(refs_dev)[None, :, None]
        rank = jnp.sum(same_dev & before, axis=2).astype(jnp.int32)
        counts = jnp.sum(chosen[:, :, None] == jnp.arange(N_BLK)[None, None, :], axis=1)
        filled = jnp.minimum(counts, CAP).astype(jnp.int32)
        scores = jax.random.randint(key_tiles, (N_BLK, N_BLK, ATILES_DEV), 0, 2 ** 20) * ATILES_DEV + jnp.arange(ATILES_DEV)[None, None, :]
        ordered = jnp.argsort(scores, axis=2)[:, :, :CAP]
        tiles = jnp.sort(ordered, axis=2).astype(jnp.int32)
        filled_pairs = jnp.transpose(filled)
        sent = jnp.where(jnp.arange(CAP)[None, None, :] < filled_pairs[:, :, None], tiles, -1)
        own_fill = jnp.take_along_axis(filled, chosen, axis=1)
        slot_pos = rank % own_fill
        receiver = jnp.broadcast_to(jnp.arange(N_BLK)[:, None], chosen.shape)
        tile_of = tiles[chosen, receiver, slot_pos]
        source = chosen * ATILES_DEV + tile_of
        return (source.astype(jnp.int32), sent.astype(jnp.int32))
    source, sent = jax.vmap(one_band)(band_keys)
    source = source.reshape(BANDS, N_BLK, OY, OX // TILE, KSRC)
    source = jnp.transpose(source, (0, 2, 1, 3, 4)).reshape(BANDS * OY, N_BLK * (OX // TILE), KSRC)
    return (source.astype(jnp.int32), sent.astype(jnp.int32))


def draw_source_tile(key, part):
    shared = routing(key)
    return shared[0]


def draw_send_tiles(key, part):
    shared = routing(key)
    return shared[1]


def draw_land_mask(key, part):
    key = jax.random.fold_in(key, 7)
    sea_cells = (jax.random.randint(key, (NY, NX), 0, 10) < 8).astype(jnp.int32)
    row_ids = jnp.arange(NY)[:, None]
    polar = (row_ids == 0) | (row_ids == NY - 1)
    return jnp.where(polar, 0, sea_cells).astype(jnp.int32)


def shard_levels(key, dims, shards, low, largest):
    level, own = 1.0, jax.random.fold_in(key, 6)
    for position, shards_of in shards:
        steps = jnp.exp(jax.random.uniform(jax.random.fold_in(own, position), (shards_of,), jnp.float32, low / len(shards), largest / len(shards)))
        level = level * jnp.repeat(steps, dims[position] // shards_of).reshape([-1 if axis == position else 1 for axis in range(len(dims))])
    return level


def noise(stream_key, shape, deviation, limit, cuts=(), held_as=jnp.bfloat16):
    entries = jax.random.normal(stream_key, shape, jnp.float32) * deviation
    if len(cuts) > 0:
        entries = shard_levels(stream_key, shape, cuts, -0.22, 0.18) * entries
    return jnp.clip(entries, min=-limit, max=limit).astype(held_as)


def setup_inputs(seed: int = 0) -> dict:
    streams_of = jax.random.split(jax.random.key(seed), 9)
    ocean_state = noise(streams_of[0], (3, NY, NX), 0.5, 4.0, ((1, 16), (2, 48)), jnp.float32)
    sea_temp = noise(streams_of[1], (NY, NX), 1.0, 6.0, ((0, 16), (1, 48)), jnp.float32)
    land_mask = draw_land_mask(jax.random.fold_in(streams_of[8], 71), 0)
    atm_flux = noise(streams_of[3], (BANDS, ATILES, FIELDS, TILE), 1.0, 6.0, ((0, 16), (1, 48)))
    remap_w = noise(streams_of[4], (NY, XTILES, KSRC, TILE, TILE), (KSRC * TILE) ** -0.5, 0.3125, ((0, 16), (1, 48)))
    source_tile = draw_source_tile(jax.random.fold_in(streams_of[8], 71), 0)
    send_tiles = draw_send_tiles(jax.random.fold_in(streams_of[8], 71), 0)
    flux_mix = noise(streams_of[7], (FORCINGS, FIELDS), FIELDS ** -0.5, 1.75, (), jnp.float32)
    return dict(ocean_state=ocean_state, sea_temp=sea_temp, land_mask=land_mask, atm_flux=atm_flux, remap_w=remap_w, source_tile=source_tile, send_tiles=send_tiles, flux_mix=flux_mix)


drag_rate = 0.02
gravity_step = 0.6
depth_step = 0.6
force_step = 0.1
spread_rate = 0.1
filter_rate = 0.1


def laplace(field):
    return jnp.roll(field, -1, axis=1) + jnp.roll(field, 1, axis=1) + jnp.roll(field, -1, axis=0) + jnp.roll(field, 1, axis=0) - 4.0 * field


def reference(ocean_state, sea_temp, land_mask, atm_flux, remap_w, source_tile, send_tiles, flux_mix):
    sea = land_mask.astype(jnp.float32)
    bands = jnp.arange(BANDS, dtype=jnp.int32)

    def forward(band):
        flux_band = lax.dynamic_index_in_dim(atm_flux, band, 0, keepdims=False)
        rows_w = lax.dynamic_slice_in_dim(remap_w, band * OY, OY, 0).astype(jnp.float32)
        rows_src = lax.dynamic_slice_in_dim(source_tile, band * OY, OY, 0)
        picked = flux_band[rows_src].astype(jnp.float32)
        remapped = jnp.einsum("ynkao,ynkfa->fyno", rows_w, picked).reshape(FIELDS, OY, NX)
        return jnp.einsum("qf,fyx->qyx", flux_mix, remapped, precision=lax.Precision.HIGHEST)

    forcing = lax.map(forward, bands)
    forcing = jnp.transpose(forcing, (1, 0, 2, 3)).reshape(FORCINGS, NY, NX)
    east_open = sea * jnp.roll(sea, -1, axis=1)
    north_open = sea * jnp.roll(sea, -1, axis=0)
    west_open = jnp.roll(east_open, 1, axis=1)
    south_open = jnp.roll(north_open, 1, axis=0)
    eta, east_vel, north_vel = ocean_state[0], ocean_state[1], ocean_state[2]
    for sub_step in range(SUBCYCLES):
        old = eta
        east_vel = east_open * ((1.0 - drag_rate) * east_vel - gravity_step * (jnp.roll(old, -1, axis=1) - old) + force_step * forcing[0])
        north_vel = north_open * ((1.0 - drag_rate) * north_vel - gravity_step * (jnp.roll(old, -1, axis=0) - old) + force_step * forcing[1])
        spread = east_open * (jnp.roll(old, -1, axis=1) - old) - west_open * (old - jnp.roll(old, 1, axis=1)) + north_open * (jnp.roll(old, -1, axis=0) - old) - south_open * (old - jnp.roll(old, 1, axis=0))
        eta = sea * (old - depth_step * (east_vel - jnp.roll(east_vel, 1, axis=1) + north_vel - jnp.roll(north_vel, 1, axis=0)) + spread_rate * spread)
        east_vel = east_open * (east_vel + filter_rate * laplace(east_vel))
        north_vel = north_open * (north_vel + filter_rate * laplace(north_vel))
    ocean_out = jnp.stack([eta, east_vel, north_vel])
    surface = sea * (sea_temp + forcing[2])
    ice_cover = sea * jax.nn.sigmoid(-2.0 * (surface + 1.0))
    returned = jnp.stack([surface, ice_cover]).astype(jnp.bfloat16)

    def backward(band):
        rows_ret = lax.dynamic_slice_in_dim(returned, band * OY, OY, 1).astype(jnp.float32).reshape(2, OY, XTILES, TILE)
        rows_w = lax.dynamic_slice_in_dim(remap_w, band * OY, OY, 0).astype(jnp.float32)
        rows_src = lax.dynamic_slice_in_dim(source_tile, band * OY, OY, 0)
        contrib = jnp.einsum("ynkao,fyno->ynkfa", rows_w, rows_ret).reshape(-1, 2, TILE)
        summed = jnp.zeros((ATILES, 2, TILE), jnp.float32).at[rows_src.reshape(-1)].add(contrib)
        listed = lax.dynamic_index_in_dim(send_tiles, band, 0, keepdims=False)
        tile_ids = jnp.arange(ATILES_DEV, dtype=jnp.int32)
        named = jnp.any(listed[:, :, :, None] == tile_ids[None, None, None, :], axis=(1, 2))
        return summed * named.reshape(ATILES).astype(jnp.float32)[:, None, None]

    atm_surface = lax.map(backward, bands)
    return ocean_out, atm_surface
```

```python
import functools

import jax
import jax.numpy as jnp
from jax import lax
from jax.experimental import pallas as pl
from jax.experimental.pallas import tpu as pltpu
from jax.sharding import PartitionSpec as P

MESH = pl.DeviceIdType.MESH

SUBCYCLES = 10
FIELDS = 12
TILE = 128
KSRC = 3
CAP = 3
OY = 16
OX = 256
ATILES_DEV = 64
N_BLK = 48
N_ROW = 16
N_SUB = 8

EXT_Y = 40
EXT_X = 384

MSG = 16
ROWS = KSRC * OY * 8

drag_rate = 0.02
gravity_step = 0.6
depth_step = 0.6
force_step = 0.1
spread_rate = 0.1
filter_rate = 0.1

f32 = jnp.float32
bf16 = jnp.bfloat16
i32 = jnp.int32


def iota(shape, dim):
    return lax.broadcasted_iota(i32, shape, dim)


def pack_sides(fields):
    width = TILE // len(fields)
    lane = iota((OY, TILE), 1) // width
    first = last = jnp.zeros((OY, TILE), f32)
    for i, field in enumerate(fields):
        head, tail = field[:, :TILE], field[:, OX - TILE :]
        if i:
            head = pltpu.roll(head, i * width, 1)
        if i + 1 < len(fields):
            tail = pltpu.roll(tail, (i + 1) * width, 1)
        first = jnp.where(lane == i, head, first)
        last = jnp.where(lane == i, tail, last)
    return first, last


def extend(own, north, south, sides, i, count):
    width = TILE // count
    lane = iota((OY, TILE), 1)

    def beside(slot):
        east, west = sides[slot], sides[3 + slot]
        if i:
            east = pltpu.roll(east, TILE - i * width, 1)
        if i + 1 < count:
            west = pltpu.roll(west, TILE - (i + 1) * width, 1)
        return jnp.where(lane < TILE // 2, east, west)

    own = jnp.concatenate([own, beside(0)], axis=1)
    north = jnp.concatenate([north, beside(1)], axis=1)
    south = jnp.concatenate([south, beside(2)], axis=1)
    between = jnp.where(iota((8, EXT_X), 0) < 4, north[8:], south[:8])
    return jnp.concatenate([own, north[:8], between, south[8:]], axis=0)


def kernel(
    state_h, temp_h, land_h, flux_h, w_h, src_s, send_s, mix_s,
    ocean_o, atm_o,
    w_v, flux_v, temp_v, land_v, own, fown,
    listing, stage, send1, recv1, send2, recv2,
    packs, fpacks, rows_in, frows_in, sides_in, fsides_in,
    idcol, pick, back, listed, lhs, fscr, rscr, cscr,
    load_sem, tile_send, tile_recv, back_send, back_recv,
    halo_send, halo_recv, fhalo_send, fhalo_recv,
):
    comp = lax.axis_index("comp")
    blk = lax.axis_index("blk")
    sub = lax.axis_index("sub")
    row = comp * N_SUB + sub

    loads = [
        pltpu.make_async_copy(src, dst, load_sem.at[i])
        for i, (src, dst) in enumerate(
            [(flux_h, flux_v), (state_h, own.at[pl.ds(0, 3)]), (land_h, land_v), (temp_h, temp_v), (w_h, w_v)]
        )
    ]
    for load in loads:
        load.start()

    def device(dx, dy):
        to_row = lax.rem(row + dy + N_ROW, N_ROW)
        return (to_row // N_SUB, lax.rem(blk + dx + N_BLK, N_BLK), lax.rem(to_row, N_SUB))

    def partner(i):
        return (comp, lax.rem(blk + i, N_BLK), sub)

    barrier = pltpu.get_barrier_semaphore()

    def greet(i, carry):
        pl.semaphore_signal(barrier, inc=1, device_id=partner(i), device_id_type=MESH)
        return carry

    lax.fori_loop(1, N_BLK, greet, 0)
    for dx, dy in ((0, 1), (0, -1), (1, 1), (1, -1), (-1, 1), (-1, -1)):
        pl.semaphore_signal(barrier, inc=1, device_id=device(dx, dy), device_id_type=MESH)

    loads[0].wait()
    mixes = []
    for q in range(3):
        total = jnp.zeros((ATILES_DEV, TILE), f32)
        for f in range(FIELDS):
            total = total + mix_s[q, f] * flux_v[f].astype(f32)
        mixes.append(total)
    high = mixes[2].astype(bf16)
    rest = (mixes[2] - high.astype(f32)).astype(bf16)
    mixed = jnp.concatenate([mixes[0].astype(bf16), mixes[1].astype(bf16), high, rest], axis=0)

    upper = iota((8, TILE), 0) < 4
    for j in range(N_BLK):
        listing[pl.ds(j * MSG, 8), :] = jnp.where(upper, send_s[0, 0, 0, j], send_s[0, 1, 0, j])
        listing[pl.ds(j * MSG + 8, 8), :] = jnp.where(upper, send_s[0, 2, 0, j], -1)
    wanted = listing[...]
    wanted = jnp.where(wanted >= 0, wanted + iota((N_BLK * MSG, TILE), 0) % 4 * ATILES_DEV, -1)
    for c in range(2):
        stage[:, c * TILE : (c + 1) * TILE] = jnp.where(
            wanted == iota((N_BLK * MSG, TILE), 1) + c * TILE, 1.0, 0.0
        ).astype(bf16)
    send1[...] = (
        jnp.dot(stage[...], mixed, preferred_element_type=f32).astype(bf16).reshape(N_BLK, MSG, TILE)
    )

    loads[1].wait()
    loads[2].wait()
    own[3] = land_v[...].astype(f32)
    packs[0], packs[1] = pack_sides([own[i] for i in range(4)])

    pl.semaphore_wait(barrier, N_BLK - 1 + 6)

    def tile_copy(i, src, dst, send_sem, recv_sem):
        to = lax.rem(blk + i, N_BLK)
        return pltpu.make_async_remote_copy(
            src_ref=src.at[to], dst_ref=dst.at[blk], send_sem=send_sem, recv_sem=recv_sem,
            device_id=partner(i), device_id_type=MESH,
        )

    def send_tile(i, carry):
        tile_copy(i, send1, recv1, tile_send, tile_recv).start()
        return carry

    lax.fori_loop(1, N_BLK, send_tile, 0)

    def halo_copies(block, pair, rows_to, sides_to, send_sem, recv_sem):
        out = []

        def add(src, dst, dx, dy):
            i = len(out)
            out.append(
                pltpu.make_async_remote_copy(
                    src_ref=src, dst_ref=dst, send_sem=send_sem.at[i], recv_sem=recv_sem.at[i],
                    device_id=device(dx, dy), device_id_type=MESH,
                )
            )

        add(block, rows_to.at[0], 0, -1)
        add(block, rows_to.at[1], 0, 1)
        for slot, dy in ((0, 0), (1, -1), (2, 1)):
            add(pair.at[0], sides_to.at[slot], -1, dy)
            add(pair.at[1], sides_to.at[3 + slot], 1, dy)
        return out

    halo = halo_copies(own, packs, rows_in, sides_in, halo_send, halo_recv)
    for copy in halo:
        copy.start()
    recv1[blk] = send1[blk]

    lane = iota((8, TILE), 1)
    line = jnp.full((1, TILE), -1, i32)
    wide = [jnp.full((1, TILE), -1, i32) for _ in range(2)]
    lane1 = iota((1, TILE), 1)
    for k in range(KSRC):
        for y in range(OY):
            left, right = src_s[k, 0, y], src_s[k, 1, y]
            idcol[pl.ds((k * OY + y) * 8, 8), :] = jnp.where(upper, left, right)
            for n, value in enumerate((left, right)):
                place = (k * OY + y) * 2 + n
                line = jnp.where(lane1 == place, value, line)
                half, start = divmod(place * 2, TILE)
                wide[half] = jnp.where(lane1 // 2 == start // 2, value, wide[half])
    ids = idcol[...]
    spot = iota((ROWS, TILE), 0) // 4
    at = iota((ROWS, TILE), 1)
    again = jnp.max(jnp.where((ids == line) & (spot < at), 1, 0), axis=0, keepdims=True)
    owners = ids // ATILES_DEV
    lower = (line // ATILES_DEV == owners) & (line < ids) & (again == 0) & (line >= 0)
    rank = jnp.dot(
        jnp.where(lower, 1.0, 0.0).astype(bf16), jnp.ones((TILE, TILE), bf16), preferred_element_type=f32
    ).astype(i32)
    target = owners * MSG + rank * 4 + iota((ROWS, TILE), 0) % 4
    for c in range(N_BLK * MSG // TILE):
        pick[:, c * TILE : (c + 1) * TILE] = jnp.where(target == at + c * TILE, 1.0, 0.0).astype(bf16)
    for c in range(2):
        mine = jnp.where(spot == (at + c * TILE) // 2, jnp.where(iota((ROWS, TILE), 0) % 4 == 0, rank, 0), 0)
        rank_line = jnp.sum(mine, axis=0, keepdims=True)
        to = (wide[c] // ATILES_DEV) * 8 + rank_line * 2 + lane1 % 2
        to = jnp.where(wide[c] >= 0, to, -1)
        back[:, c * TILE : (c + 1) * TILE] = jnp.where(to == iota((N_BLK * 8, TILE), 0), 1.0, 0.0).astype(bf16)
    for c in range(3):
        tile_line = jnp.full((1, TILE), -1, i32)
        for j in range(16):
            for s in range(CAP):
                tile_line = jnp.where(lane1 // 2 == j * 4 + s, send_s[0, s, 0, c * 16 + j], tile_line)
        tile_line = tile_line * 2 + lane1 % 2
        listed[:, c * TILE : (c + 1) * TILE] = jnp.where(
            tile_line == iota((2 * ATILES_DEV, TILE), 0), 1.0, 0.0
        ).astype(bf16)
    rscr[...] = jnp.zeros_like(rscr)

    others = pl.ds(0, N_BLK - 1)
    pltpu.make_async_copy(send1.at[others], recv1.at[others], tile_recv).wait()

    picked = jnp.dot(
        pick[...], recv1[...].reshape(N_BLK * MSG, TILE), preferred_element_type=f32
    ).astype(bf16)
    lhs[...] = jnp.concatenate([picked[k * TILE : (k + 1) * TILE] for k in range(KSRC)], axis=1)
    loads[4].wait()

    def weights(y):
        return jnp.concatenate([w_v[y, n].reshape(KSRC * TILE, TILE) for n in range(2)], axis=1)

    for y in range(OY):
        out = jnp.dot(lhs[pl.ds(y // 2 * 16, 16), :], weights(y), preferred_element_type=f32)
        for n in range(2):
            fscr[pl.ds(n * TILE + y * 8, 8), :] = out[y % 2 * 8 : y % 2 * 8 + 8, n * TILE : (n + 1) * TILE]

    def forcing(q):
        return jnp.concatenate(
            [fscr[pl.ds(n * TILE + 4 * n + q, OY, stride=8), :] for n in range(2)], axis=1
        )

    fown[0], fown[1] = forcing(0), forcing(1)
    fpacks[0], fpacks[1] = pack_sides([fown[0], fown[1]])
    fhalo = halo_copies(fown, fpacks, frows_in, fsides_in, fhalo_send, fhalo_recv)
    for copy in fhalo:
        copy.start()

    loads[3].wait()
    sea = own[3]
    surface = sea * (temp_v[...] + (forcing(2) + forcing(3)))
    ice = sea * jax.nn.sigmoid(-2.0 * (surface + 1.0))
    for f, field in enumerate((surface, ice)):
        field = field.astype(bf16).astype(f32)
        for n in range(2):
            rscr[pl.ds(n * 4 * OY + 2 * n + f, OY, stride=4), :] = field[:, n * TILE : (n + 1) * TILE]
    returned = jnp.concatenate([rscr[: 4 * OY], rscr[4 * OY :]], axis=1).astype(bf16)
    for y in range(OY):
        out = lax.dot_general(
            returned[y // 4 * 16 : y // 4 * 16 + 16], weights(y), (((1,), (1,)), ((), ())),
            preferred_element_type=f32,
        )
        cscr[pl.ds(y * 4, 4), :] = out[y % 4 * 4 : y % 4 * 4 + 4]
    terms = jnp.concatenate([cscr[:, k * TILE : (k + 1) * TILE] for k in range(KSRC)], axis=0)

    def routed(table, rows):
        top = rows.astype(bf16)
        rest = (rows - top.astype(f32)).astype(bf16)
        return jnp.dot(table, top, preferred_element_type=f32) + jnp.dot(table, rest, preferred_element_type=f32)

    send2[...] = routed(back[:, : 4 * OY * KSRC], terms).reshape(N_BLK, 8, TILE)

    def send_back(i, carry):
        tile_copy(i, send2, recv2, back_send, back_recv).start()
        return carry

    lax.fori_loop(1, N_BLK, send_back, 0)
    recv2[blk] = send2[blk]

    for copy in halo:
        copy.wait_recv()
    around = [
        extend(own[i], rows_in[0, i], rows_in[1, i], [sides_in[j] for j in range(6)], i, 4) for i in range(4)
    ]
    eta, east, north, sea = around
    east_open = sea * pltpu.roll(sea, EXT_X - 1, 1)
    north_open = sea * pltpu.roll(sea, EXT_Y - 1, 0)

    for copy in fhalo:
        copy.wait_recv()
    push = [
        extend(fown[i], frows_in[0, i], frows_in[1, i], [fsides_in[j] for j in range(6)], i, 2) for i in range(2)
    ]
    push_east = force_step * east_open * push[0]
    push_north = force_step * north_open * push[1]

    def from_east(x):
        return pltpu.roll(x, EXT_X - 1, 1)

    def from_west(x):
        return pltpu.roll(x, 1, 1)

    def from_north(x):
        return pltpu.roll(x, EXT_Y - 1, 0)

    def from_south(x):
        return pltpu.roll(x, 1, 0)

    def advance(_, carried):
        eta, east, north = carried
        slope_east = east_open * (from_east(eta) - eta)
        slope_north = north_open * (from_north(eta) - eta)
        east = (1.0 - drag_rate) * east_open * east - gravity_step * slope_east + push_east
        north = (1.0 - drag_rate) * north_open * north - gravity_step * slope_north + push_north
        flow_east = depth_step * east - spread_rate * slope_east
        flow_north = depth_step * north - spread_rate * slope_north
        eta = sea * (eta - (flow_east - from_west(flow_east)) - (flow_north - from_south(flow_north)))

        def smooth(x):
            around = from_east(x) + from_west(x) + from_north(x) + from_south(x)
            return (1.0 - 4.0 * filter_rate) * x + filter_rate * around

        return eta, east_open * smooth(east), north_open * smooth(north)

    final = lax.fori_loop(0, SUBCYCLES, advance, (eta, east, north))
    for i in range(3):
        ocean_o[i] = final[i][:OY, :OX]

    pltpu.make_async_copy(send2.at[others], recv2.at[others], back_recv).wait()
    atm_o[...] = routed(listed[...], recv2[...].reshape(N_BLK * 8, TILE))

    pltpu.make_async_copy(send1.at[others], recv1.at[others], tile_send).wait()
    pltpu.make_async_copy(send2.at[others], recv2.at[others], back_send).wait()
    for copy in halo + fhalo:
        copy.wait_send()


def shards(ocean_state, sea_temp, land_mask, atm_flux, remap_w, source_tile, send_tiles, flux_mix):
    hbm = pl.BlockSpec(memory_space=pl.ANY)
    smem = pl.BlockSpec(memory_space=pltpu.SMEM)
    vmem = pl.BlockSpec(memory_space=pltpu.VMEM)
    ocean, atm = pl.pallas_call(
        kernel,
        out_shape=(
            jax.ShapeDtypeStruct((3, OY, OX), f32),
            jax.ShapeDtypeStruct((2 * ATILES_DEV, TILE), f32),
        ),
        in_specs=[hbm] * 5 + [smem] * 3,
        out_specs=(vmem, vmem),
        scratch_shapes=[
            pltpu.VMEM((OY, 2, KSRC, TILE, TILE), bf16),
            pltpu.VMEM((FIELDS, ATILES_DEV, TILE), bf16),
            pltpu.VMEM((OY, OX), f32),
            pltpu.VMEM((OY, OX), i32),
            pltpu.VMEM((4, OY, OX), f32),
            pltpu.VMEM((2, OY, OX), f32),
            pltpu.VMEM((N_BLK * MSG, TILE), i32),
            pltpu.VMEM((N_BLK * MSG, 4 * ATILES_DEV), bf16),
            pltpu.VMEM((N_BLK, MSG, TILE), bf16),
            pltpu.VMEM((N_BLK, MSG, TILE), bf16),
            pltpu.VMEM((N_BLK, 8, TILE), f32),
            pltpu.VMEM((N_BLK, 8, TILE), f32),
            pltpu.VMEM((2, OY, TILE), f32),
            pltpu.VMEM((2, OY, TILE), f32),
            pltpu.VMEM((2, 4, OY, OX), f32),
            pltpu.VMEM((2, 2, OY, OX), f32),
            pltpu.VMEM((6, OY, TILE), f32),
            pltpu.VMEM((6, OY, TILE), f32),
            pltpu.VMEM((ROWS, TILE), i32),
            pltpu.VMEM((ROWS, N_BLK * MSG), bf16),
            pltpu.VMEM((N_BLK * 8, 2 * TILE), bf16),
            pltpu.VMEM((2 * ATILES_DEV, N_BLK * 8), bf16),
            pltpu.VMEM((TILE, KSRC * TILE), bf16),
            pltpu.VMEM((2 * TILE, TILE), f32),
            pltpu.VMEM((8 * OY, TILE), f32),
            pltpu.VMEM((4 * OY, KSRC * TILE), f32),
            pltpu.SemaphoreType.DMA((5,)),
            pltpu.SemaphoreType.DMA,
            pltpu.SemaphoreType.DMA,
            pltpu.SemaphoreType.DMA,
            pltpu.SemaphoreType.DMA,
            pltpu.SemaphoreType.DMA((8,)),
            pltpu.SemaphoreType.DMA((8,)),
            pltpu.SemaphoreType.DMA((8,)),
            pltpu.SemaphoreType.DMA((8,)),
        ],
        compiler_params=pltpu.CompilerParams(
            collective_id=0, has_side_effects=True, vmem_limit_bytes=60 * 1024 * 1024
        ),
    )(
        ocean_state, sea_temp, land_mask,
        jnp.transpose(atm_flux[0], (1, 0, 2)),
        remap_w,
        jnp.transpose(source_tile, (2, 1, 0)),
        jnp.transpose(send_tiles, (0, 3, 1, 2)),
        flux_mix,
    )
    return ocean, atm.reshape(1, ATILES_DEV, 2, TILE)


def solution(mesh):
    placed = (
        P(None, ("comp", "sub"), "blk"),
        P(("comp", "sub"), "blk"),
        P(("comp", "sub"), "blk"),
        P(("comp", "sub"), "blk", None, None),
        P(("comp", "sub"), "blk", None, None, None),
        P(("comp", "sub"), "blk", None),
        P(("comp", "sub"), "blk", None, None),
        P(),
    )
    return jax.shard_map(
        shards,
        mesh=mesh,
        in_specs=placed,
        out_specs=(P(None, ("comp", "sub"), "blk"), P(("comp", "sub"), "blk", None, None)),
        check_vma=False,
    )
```

```python
import functools

import jax
import jax.numpy as jnp
from jax import lax
from jax.experimental import pallas as pl
from jax.experimental.pallas import tpu as pltpu
from jax.sharding import PartitionSpec as P

MESH = pl.DeviceIdType.MESH

SUBCYCLES = 10
FIELDS = 12
TILE = 128
KSRC = 3
CAP = 3
OY = 16
OX = 256
ATILES_DEV = 64
N_BLK = 48
N_ROW = 16
N_SUB = 8

EXT_Y = 40
EXT_X = 384

MSG = 8
REFS = KSRC * 2 * OY

drag_rate = 0.02
gravity_step = 0.6
depth_step = 0.6
force_step = 0.1
spread_rate = 0.1
filter_rate = 0.1

f32 = jnp.float32
bf16 = jnp.bfloat16
i32 = jnp.int32


def iota(shape, dim):
    return lax.broadcasted_iota(i32, shape, dim)


def pack_sides(fields):
    width = TILE // len(fields)
    lane = iota((OY, TILE), 1) // width
    first = last = jnp.zeros((OY, TILE), f32)
    for i, field in enumerate(fields):
        head, tail = field[:, :TILE], field[:, OX - TILE :]
        if i:
            head = pltpu.roll(head, i * width, 1)
        if i + 1 < len(fields):
            tail = pltpu.roll(tail, (i + 1) * width, 1)
        first = jnp.where(lane == i, head, first)
        last = jnp.where(lane == i, tail, last)
    return first, last


def extend(own, north, south, sides, i, count):
    width = TILE // count
    lane = iota((OY, TILE), 1)

    def beside(slot):
        east, west = sides[slot], sides[3 + slot]
        if i:
            east = pltpu.roll(east, TILE - i * width, 1)
        if i + 1 < count:
            west = pltpu.roll(west, TILE - (i + 1) * width, 1)
        return jnp.where(lane < TILE // 2, east, west)

    own = jnp.concatenate([own, beside(0)], axis=1)
    north = jnp.concatenate([north, beside(1)], axis=1)
    south = jnp.concatenate([south, beside(2)], axis=1)
    between = jnp.where(iota((8, EXT_X), 0) < 4, north[8:], south[:8])
    return jnp.concatenate([own, north[:8], between, south[8:]], axis=0)


def stage_tiles(flux_v, send_s, mix_s, listing, stage, send_a, send_b):
    mixes = []
    for q in range(3):
        total = jnp.zeros((ATILES_DEV, TILE), f32)
        for f in range(FIELDS):
            total = total + mix_s[q, f] * flux_v[f].astype(f32)
        mixes.append(total)
    high = mixes[2].astype(bf16)
    rest = (mixes[2] - high.astype(f32)).astype(bf16)

    line = iota((8, TILE), 0)
    takes = [(line == s) | (line == s + CAP) for s in range(CAP)]
    for j in range(N_BLK):
        tiles = jnp.full((8, TILE), -1, i32)
        for s in range(CAP):
            tiles = jnp.where(takes[s], send_s[0, s, 0, j], tiles)
        listing[pl.ds(j * MSG, MSG), :] = tiles
    wanted = listing[...]
    second = iota((N_BLK * MSG, TILE), 0) % MSG >= CAP
    wanted = jnp.where(wanted >= 0, wanted + jnp.where(second, ATILES_DEV, 0), -1)
    stage[...] = jnp.where(wanted == iota((N_BLK * MSG, TILE), 1), 1.0, 0.0).astype(bf16)
    for parts, send in (((high, rest), send_a), ((mixes[0].astype(bf16), mixes[1].astype(bf16)), send_b)):
        rows = jnp.dot(stage[...], jnp.concatenate(parts, axis=0), preferred_element_type=f32)
        send[...] = rows.astype(bf16).reshape(N_BLK, MSG, TILE)


def tables(src_s, send_s, idcol, pick, back, listed):
    line = iota((8, TILE), 0)
    refs = jnp.full((1, TILE), -1, i32)
    wide = [jnp.full((1, TILE), -1, i32) for _ in range(2)]
    lane1 = iota((1, TILE), 1)
    for k in range(KSRC):
        for n in range(2):
            for half in range(2):
                column = jnp.full((8, TILE), -1, i32)
                for i in range(8):
                    y = half * 8 + i
                    value = src_s[k, n, y]
                    place = (k * 2 + n) * OY + y
                    column = jnp.where(line == i, value, column)
                    refs = jnp.where(lane1 == place, value, refs)
                    pair = k * 32 + y * 2 + n
                    wide[pair // 64] = jnp.where(lane1 // 2 == pair % 64, value, wide[pair // 64])
                idcol[pl.ds((k * 2 + n) * OY + half * 8, 8), :] = column
    ids = idcol[...]
    spot = iota((REFS, TILE), 0)
    at = iota((REFS, TILE), 1)
    again = jnp.max(jnp.where((ids == refs) & (spot < at), 1, 0), axis=0, keepdims=True)
    owners = ids // ATILES_DEV
    lower = (refs // ATILES_DEV == owners) & (refs < ids) & (again == 0) & (refs >= 0)
    rank = jnp.dot(
        jnp.where(lower, 1.0, 0.0).astype(bf16), jnp.ones((TILE, TILE), bf16), preferred_element_type=f32
    ).astype(i32)
    target = owners * MSG + rank
    for c in range(N_BLK * MSG // TILE):
        for p in range(2):
            hit = jnp.where(target + p * CAP == at + c * TILE, 1.0, 0.0).astype(bf16)
            for k in range(KSRC):
                pick[pl.ds((k * 2 + p) * 32, 32), c * TILE : (c + 1) * TILE] = hit[k * 32 : (k + 1) * 32]
    order = spot // 32 * 32 + spot % OY * 2 + spot // OY % 2
    for c in range(2):
        rank_line = jnp.sum(jnp.where(order == at // 2 + c * 64, rank, 0), axis=0, keepdims=True)
        to = (wide[c] // ATILES_DEV) * MSG + rank_line * 2 + lane1 % 2
        to = jnp.where(wide[c] >= 0, to, -1)
        back[:, c * TILE : (c + 1) * TILE] = jnp.where(to == iota((N_BLK * MSG, TILE), 0), 1.0, 0.0).astype(bf16)
    for c in range(3):
        tile_line = jnp.full((1, TILE), -1, i32)
        for j in range(16):
            for s in range(CAP):
                tile_line = jnp.where(lane1 // 2 == j * 4 + s, send_s[0, s, 0, c * 16 + j], tile_line)
        tile_line = tile_line * 2 + lane1 % 2
        listed[:, c * TILE : (c + 1) * TILE] = jnp.where(
            tile_line == iota((2 * ATILES_DEV, TILE), 0), 1.0, 0.0
        ).astype(bf16)


def weights(w_v, y):
    return jnp.concatenate([w_v[y, n].reshape(KSRC * TILE, TILE) for n in range(2)], axis=1)


def turn_weights(w_v, wt_v):
    for y in range(OY):
        wt_v[y] = weights(w_v, y).T


def remap(pick, recv, lhs, w_v):
    picked = jnp.dot(
        pick[...], recv[...].reshape(N_BLK * MSG, TILE), preferred_element_type=f32
    ).astype(bf16)
    lhs[...] = jnp.concatenate([picked[k * 64 : (k + 1) * 64] for k in range(KSRC)], axis=1)
    row = iota((OY, TILE), 0)
    parts = [[jnp.zeros((OY, TILE), f32) for _ in range(2)] for _ in range(2)]
    for y in range(OY):
        out = jnp.dot(lhs[...], weights(w_v, y), preferred_element_type=f32)
        for p in range(2):
            for n in range(2):
                rows = out[(p * 2 + n) * OY : (p * 2 + n + 1) * OY, n * TILE : (n + 1) * TILE]
                parts[p][n] = jnp.where(row == y, rows, parts[p][n])
    return [jnp.concatenate(part, axis=1) for part in parts]


def remap_back(sea, temp, push, wt_v, rscr, cscr, back, send2):
    surface = sea * (temp + push)
    ice = sea * jax.nn.sigmoid(-2.0 * (surface + 1.0))
    for f, field in enumerate((surface, ice)):
        field = field.astype(bf16).astype(f32)
        for n in range(2):
            rscr[pl.ds(n * 4 * OY + 2 * n + f, OY, stride=4), :] = field[:, n * TILE : (n + 1) * TILE]
    returned = jnp.concatenate([rscr[: 4 * OY], rscr[4 * OY :]], axis=1).astype(bf16)
    for y in range(OY):
        out = jnp.dot(returned[y // 4 * 16 : y // 4 * 16 + 16], wt_v[y], preferred_element_type=f32)
        cscr[pl.ds(y * 4, 4), :] = out[y % 4 * 4 : y % 4 * 4 + 4]
    terms = jnp.concatenate([cscr[:, k * TILE : (k + 1) * TILE] for k in range(KSRC)], axis=0)
    table = back[:, : 4 * OY * KSRC]
    top = terms.astype(bf16)
    rest = (terms - top.astype(f32)).astype(bf16)
    sums = jnp.dot(table, top, preferred_element_type=f32) + jnp.dot(table, rest, preferred_element_type=f32)
    send2[...] = sums.astype(bf16).reshape(N_BLK, MSG, TILE)


def gather_back(listed, recv2, atm_o):
    atm_o[...] = jnp.dot(listed[...], recv2[...].reshape(N_BLK * MSG, TILE), preferred_element_type=f32)


def subcycles(around, push, ocean_o):
    eta, east, north, sea = around
    east_open = sea * pltpu.roll(sea, EXT_X - 1, 1)
    north_open = sea * pltpu.roll(sea, EXT_Y - 1, 0)

    push_east = force_step * east_open * push[0]
    push_north = force_step * north_open * push[1]

    def from_east(x):
        return pltpu.roll(x, EXT_X - 1, 1)

    def from_west(x):
        return pltpu.roll(x, 1, 1)

    def from_north(x):
        return pltpu.roll(x, EXT_Y - 1, 0)

    def from_south(x):
        return pltpu.roll(x, 1, 0)

    def advance(_, carried):
        eta, east, north = carried
        slope_east = east_open * (from_east(eta) - eta)
        slope_north = north_open * (from_north(eta) - eta)
        east = (1.0 - drag_rate) * east_open * east - gravity_step * slope_east + push_east
        north = (1.0 - drag_rate) * north_open * north - gravity_step * slope_north + push_north
        flow_east = depth_step * east - spread_rate * slope_east
        flow_north = depth_step * north - spread_rate * slope_north
        eta = sea * (eta - (flow_east - from_west(flow_east)) - (flow_north - from_south(flow_north)))

        def smooth(x):
            around = from_east(x) + from_west(x) + from_north(x) + from_south(x)
            return (1.0 - 4.0 * filter_rate) * x + filter_rate * around

        return eta, east_open * smooth(east), north_open * smooth(north)

    final = lax.fori_loop(0, SUBCYCLES, advance, (eta, east, north))
    for i in range(3):
        ocean_o[i] = final[i][:OY, :OX]


def kernel(
    state_h, temp_h, land_h, flux_h, w_h, src_h, send_h, mix_h,
    ocean_o, atm_o,
    src_s, send_s, mix_s,
    w_v, wt_v, flux_v, temp_v, land_v, own, fown,
    listing, stage, send_a, recv_a, send_b, recv_b, send2, recv2,
    packs, fpacks, rows_in, frows_in, sides_in, fsides_in,
    idcol, pick, back, listed, lhs, rscr, cscr,
    load_sem, a_send, a_recv, b_send, b_recv, back_send, back_recv,
    halo_send, halo_recv, fhalo_send, fhalo_recv,
):
    comp = lax.axis_index("comp")
    blk = lax.axis_index("blk")
    sub = lax.axis_index("sub")
    row = comp * N_SUB + sub

    def device(dx, dy):
        to_row = lax.rem(row + dy + N_ROW, N_ROW)
        return (to_row // N_SUB, lax.rem(blk + dx + N_BLK, N_BLK), lax.rem(to_row, N_SUB))

    def partner(i):
        return (comp, lax.rem(blk + i, N_BLK), sub)

    loads = [
        pltpu.make_async_copy(src, dst, load_sem.at[i])
        for i, (src, dst) in enumerate(
            [
                (mix_h, mix_s), (flux_h, flux_v), (send_h, send_s), (src_h, src_s),
                (state_h, own.at[pl.ds(0, 3)]), (land_h, land_v), (temp_h, temp_v), (w_h, w_v),
            ]
        )
    ]
    for load in loads:
        load.start()

    barrier = pltpu.get_barrier_semaphore()

    def greet(i, carry):
        pl.semaphore_signal(barrier, inc=1, device_id=partner(i), device_id_type=MESH)
        return carry

    lax.fori_loop(1, N_BLK, greet, 0)
    for dx, dy in ((0, 1), (0, -1), (1, 1), (1, -1), (-1, 1), (-1, -1)):
        pl.semaphore_signal(barrier, inc=1, device_id=device(dx, dy), device_id_type=MESH)

    for load in loads[:3]:
        load.wait()
    stage_tiles(flux_v, send_s, mix_s, listing, stage, send_a, send_b)

    pl.semaphore_wait(barrier, N_BLK - 1 + 6)

    def send_all(src, dst, send_sem, recv_sem):
        def send(i, carry):
            pltpu.make_async_remote_copy(
                src_ref=src.at[lax.rem(blk + i, N_BLK)], dst_ref=dst.at[blk],
                send_sem=send_sem, recv_sem=recv_sem,
                device_id=partner(i), device_id_type=MESH,
            ).start()
            return carry

        lax.fori_loop(1, N_BLK, send, 0)

    others = pl.ds(0, N_BLK - 1)

    def all_of(src, dst, sem):
        return pltpu.make_async_copy(src.at[others], dst.at[others], sem)

    send_all(send_a, recv_a, a_send, a_recv)
    send_all(send_b, recv_b, b_send, b_recv)

    def halo_copies(block, pair, rows_to, sides_to, send_sem, recv_sem):
        out = []

        def add(src, dst, dx, dy):
            i = len(out)
            out.append(
                pltpu.make_async_remote_copy(
                    src_ref=src, dst_ref=dst, send_sem=send_sem.at[i], recv_sem=recv_sem.at[i],
                    device_id=device(dx, dy), device_id_type=MESH,
                )
            )

        add(block, rows_to.at[0], 0, -1)
        add(block, rows_to.at[1], 0, 1)
        for slot, dy in ((0, 0), (1, -1), (2, 1)):
            add(pair.at[0], sides_to.at[slot], -1, dy)
            add(pair.at[1], sides_to.at[3 + slot], 1, dy)
        return out

    loads[4].wait()
    loads[5].wait()
    own[3] = land_v[...].astype(f32)
    packs[0], packs[1] = pack_sides([own[i] for i in range(4)])
    halo = halo_copies(own, packs, rows_in, sides_in, halo_send, halo_recv)
    for copy in halo:
        copy.start()
    recv_a[blk] = send_a[blk]
    recv_b[blk] = send_b[blk]

    loads[3].wait()
    tables(src_s, send_s, idcol, pick, back, listed)
    rscr[...] = jnp.zeros_like(rscr)
    loads[6].wait()
    loads[7].wait()
    turn_weights(w_v, wt_v)

    all_of(send_a, recv_a, a_recv).wait()
    push = remap(pick, recv_a, lhs, w_v)
    remap_back(own[3], temp_v[...], push[0] + push[1], wt_v, rscr, cscr, back, send2)
    send_all(send2, recv2, back_send, back_recv)
    recv2[blk] = send2[blk]

    all_of(send_b, recv_b, b_recv).wait()
    fown[0], fown[1] = remap(pick, recv_b, lhs, w_v)
    fpacks[0], fpacks[1] = pack_sides([fown[0], fown[1]])
    fhalo = halo_copies(fown, fpacks, frows_in, fsides_in, fhalo_send, fhalo_recv)
    for copy in fhalo:
        copy.start()

    for copy in halo:
        copy.wait_recv()
    around = [
        extend(own[i], rows_in[0, i], rows_in[1, i], [sides_in[j] for j in range(6)], i, 4) for i in range(4)
    ]
    for copy in fhalo:
        copy.wait_recv()
    push = [
        extend(fown[i], frows_in[0, i], frows_in[1, i], [fsides_in[j] for j in range(6)], i, 2) for i in range(2)
    ]
    subcycles(around, push, ocean_o)

    all_of(send2, recv2, back_recv).wait()
    gather_back(listed, recv2, atm_o)

    all_of(send_a, recv_a, a_send).wait()
    all_of(send_b, recv_b, b_send).wait()
    all_of(send2, recv2, back_send).wait()
    for copy in halo + fhalo:
        copy.wait_send()


def shards(ocean_state, sea_temp, land_mask, atm_flux, remap_w, source_tile, send_tiles, flux_mix):
    hbm = pl.BlockSpec(memory_space=pltpu.HBM)
    vmem = pl.BlockSpec(memory_space=pltpu.VMEM)
    message = pltpu.VMEM((N_BLK, MSG, TILE), bf16)
    dma = pltpu.SemaphoreType.DMA
    ocean, atm = pl.pallas_call(
        kernel,
        out_shape=(
            jax.ShapeDtypeStruct((3, OY, OX), f32),
            jax.ShapeDtypeStruct((2 * ATILES_DEV, TILE), f32),
        ),
        in_specs=[hbm] * 8,
        out_specs=(vmem, vmem),
        scratch_shapes=[
            pltpu.SMEM((KSRC, 2, OY), i32),
            pltpu.SMEM((1, CAP, 1, N_BLK), i32),
            pltpu.SMEM((3, FIELDS), f32),
            pltpu.VMEM((OY, 2, KSRC, TILE, TILE), bf16),
            pltpu.VMEM((OY, OX, KSRC * TILE), bf16),
            pltpu.VMEM((FIELDS, ATILES_DEV, TILE), bf16),
            pltpu.VMEM((OY, OX), f32),
            pltpu.VMEM((OY, OX), i32),
            pltpu.VMEM((4, OY, OX), f32),
            pltpu.VMEM((2, OY, OX), f32),
            pltpu.VMEM((N_BLK * MSG, TILE), i32),
            pltpu.VMEM((N_BLK * MSG, 2 * ATILES_DEV), bf16),
            message, message, message, message, message, message,
            pltpu.VMEM((2, OY, TILE), f32),
            pltpu.VMEM((2, OY, TILE), f32),
            pltpu.VMEM((2, 4, OY, OX), f32),
            pltpu.VMEM((2, 2, OY, OX), f32),
            pltpu.VMEM((6, OY, TILE), f32),
            pltpu.VMEM((6, OY, TILE), f32),
            pltpu.VMEM((REFS, TILE), i32),
            pltpu.VMEM((2 * REFS, N_BLK * MSG), bf16),
            pltpu.VMEM((N_BLK * MSG, 2 * TILE), bf16),
            pltpu.VMEM((2 * ATILES_DEV, N_BLK * MSG), bf16),
            pltpu.VMEM((4 * OY, KSRC * TILE), bf16),
            pltpu.VMEM((8 * OY, TILE), f32),
            pltpu.VMEM((4 * OY, KSRC * TILE), f32),
            dma((8,)),
            dma, dma, dma, dma, dma, dma,
            dma((8,)), dma((8,)), dma((8,)), dma((8,)),
        ],
        compiler_params=pltpu.CompilerParams(
            collective_id=0, has_side_effects=True, vmem_limit_bytes=32 * 1024 * 1024
        ),
    )(
        *(
            pltpu.with_memory_space_constraint(x, pltpu.HBM)
            for x in (
                ocean_state, sea_temp, land_mask,
                jnp.transpose(atm_flux[0], (1, 0, 2)),
                remap_w,
                jnp.transpose(source_tile, (2, 1, 0)),
                jnp.transpose(send_tiles, (0, 3, 1, 2)),
                flux_mix,
            )
        )
    )
    return ocean, atm.reshape(1, ATILES_DEV, 2, TILE)


def solution(mesh):
    placed = (
        P(None, ("comp", "sub"), "blk"),
        P(("comp", "sub"), "blk"),
        P(("comp", "sub"), "blk"),
        P(("comp", "sub"), "blk", None, None),
        P(("comp", "sub"), "blk", None, None, None),
        P(("comp", "sub"), "blk", None),
        P(("comp", "sub"), "blk", None, None),
        P(),
    )
    return jax.shard_map(
        shards,
        mesh=mesh,
        in_specs=placed,
        out_specs=(P(None, ("comp", "sub"), "blk"), P(("comp", "sub"), "blk", None, None)),
        check_vma=False,
    )
```

```python
import functools

import jax
import jax.numpy as jnp
from jax import lax
from jax.experimental import pallas as pl
from jax.experimental.pallas import tpu as pltpu
from jax.sharding import PartitionSpec as P

MESH = pl.DeviceIdType.MESH

SUBCYCLES = 10
FIELDS = 12
TILE = 128
KSRC = 3
CAP = 3
OY = 16
OX = 256
ATILES_DEV = 64
N_BLK = 48
N_ROW = 16
N_SUB = 8

EXT_Y = 40
EXT_X = 384
PLANES = EXT_Y // 8
COLUMNS = EXT_X // TILE

PARTS = 4
MSG = CAP * PARTS
RET = CAP * 2
REFS = KSRC * OY * 2
ROWS = REFS * PARTS

drag_rate = 0.02
gravity_step = 0.6
depth_step = 0.6
force_step = 0.1
spread_rate = 0.1
filter_rate = 0.1

f32 = jnp.float32
bf16 = jnp.bfloat16
i32 = jnp.int32


def iota(shape, dim):
    return lax.broadcasted_iota(i32, shape, dim)


def pack_sides(fields):
    width = TILE // len(fields)
    lane = iota((OY, TILE), 1) // width
    first = last = jnp.zeros((OY, TILE), f32)
    for i, field in enumerate(fields):
        head, tail = field[:, :TILE], field[:, OX - TILE :]
        if i:
            head = pltpu.roll(head, i * width, 1)
        if i + 1 < len(fields):
            tail = pltpu.roll(tail, (i + 1) * width, 1)
        first = jnp.where(lane == i, head, first)
        last = jnp.where(lane == i, tail, last)
    return first, last


def extend(own, north, south, sides, i, count):
    width = TILE // count
    lane = iota((OY, TILE), 1)

    def beside(slot):
        east, west = sides[slot], sides[3 + slot]
        if i:
            east = pltpu.roll(east, TILE - i * width, 1)
        if i + 1 < count:
            west = pltpu.roll(west, TILE - (i + 1) * width, 1)
        return jnp.where(lane < TILE // 2, east, west)

    own = jnp.concatenate([own, beside(0)], axis=1)
    north = jnp.concatenate([north, beside(1)], axis=1)
    south = jnp.concatenate([south, beside(2)], axis=1)
    between = jnp.where(iota((8, EXT_X), 0) < 4, north[8:], south[:8])
    return jnp.concatenate([own, north[:8], between, south[8:]], axis=0)


def stage_tiles(flux_v, send_s, mix_s, listing, stage, send1):
    mixes = []
    for q in range(3):
        total = jnp.zeros((ATILES_DEV, TILE), f32)
        for f in range(FIELDS):
            total = total + mix_s[q, f] * flux_v[f].astype(f32)
        mixes.append(total)
    high = mixes[2].astype(bf16)
    rest = (mixes[2] - high.astype(f32)).astype(bf16)
    mixed = jnp.concatenate([mixes[0].astype(bf16), mixes[1].astype(bf16), high, rest], axis=0)

    upper = iota((8, TILE), 0) < PARTS
    for j in range(0, N_BLK, 2):
        slots = [send_s[0, s, 0, i] for i in (j, j + 1) for s in range(CAP)]
        for i in range(CAP):
            listing[pl.ds(j * MSG + i * 8, 8), :] = jnp.where(upper, slots[2 * i], slots[2 * i + 1])
    wanted = listing[...]
    part = iota((N_BLK * MSG, TILE), 0) % PARTS
    wanted = jnp.where(wanted >= 0, wanted + part * ATILES_DEV, -1)
    for c in range(2):
        stage[:, c * TILE : (c + 1) * TILE] = jnp.where(
            wanted == iota((N_BLK * MSG, TILE), 1) + c * TILE, 1.0, 0.0
        ).astype(bf16)
    rows = jnp.dot(stage[...], mixed, preferred_element_type=f32).astype(bf16)
    send1[...] = rows.reshape(send1.shape)


def tables(src_s, send_s, idcol, pick, back, listed):
    upper = iota((8, TILE), 0) < PARTS
    refs = jnp.full((1, TILE), -1, i32)
    wide = [jnp.full((1, TILE), -1, i32) for _ in range(2)]
    lane1 = iota((1, TILE), 1)
    for k in range(KSRC):
        for y in range(OY):
            both = [src_s[k, n, y] for n in range(2)]
            idcol[pl.ds((k * OY + y) * 8, 8), :] = jnp.where(upper, both[0], both[1])
            for n, value in enumerate(both):
                place = (k * OY + y) * 2 + n
                refs = jnp.where(lane1 == place, value, refs)
                wide[place // 64] = jnp.where(lane1 // 2 == place % 64, value, wide[place // 64])
    ids = idcol[...]
    spot = iota((ROWS, TILE), 0) // PARTS
    part = iota((ROWS, TILE), 0) % PARTS
    at = iota((ROWS, TILE), 1)
    again = jnp.max(jnp.where((ids == refs) & (spot < at), 1, 0), axis=0, keepdims=True)
    owners = ids // ATILES_DEV
    lower = (refs // ATILES_DEV == owners) & (refs < ids) & (again == 0) & (refs >= 0)
    rank = jnp.dot(
        jnp.where(lower, 1.0, 0.0).astype(bf16), jnp.ones((TILE, TILE), bf16), preferred_element_type=f32
    ).astype(i32)
    target = owners * MSG + rank * PARTS + part
    for c in range(0, N_BLK * MSG, TILE):
        width = min(TILE, N_BLK * MSG - c)
        pick[:, c : c + width] = jnp.where(target == at + c, 1.0, 0.0).astype(bf16)[:, :width]
    first = jnp.where(part == 0, rank, 0)
    for c in range(2):
        rank_line = jnp.sum(jnp.where(spot == at // 2 + c * 64, first, 0), axis=0, keepdims=True)
        to = (wide[c] // ATILES_DEV) * RET + rank_line * 2 + lane1 % 2
        to = jnp.where(wide[c] >= 0, to, -1)
        back[:, c * TILE : (c + 1) * TILE] = jnp.where(to == iota((N_BLK * RET, TILE), 0), 1.0, 0.0).astype(bf16)
    slot = [jnp.full((1, TILE), -1, i32) for _ in range(3)]
    for j in range(N_BLK):
        for s in range(CAP):
            place = j * CAP + s
            slot[place // 64] = jnp.where(lane1 // 2 == place % 64, send_s[0, s, 0, j], slot[place // 64])
    for c in range(3):
        width = min(TILE, N_BLK * RET - c * TILE)
        hit = slot[c] * 2 + lane1 % 2 == iota((2 * ATILES_DEV, TILE), 0)
        listed[:, c * TILE : c * TILE + width] = jnp.where(hit, 1.0, 0.0).astype(bf16)[:, :width]


def weights(w_v, y):
    return jnp.concatenate([w_v[y, n].reshape(KSRC * TILE, TILE) for n in range(2)], axis=1)


def turn_weights(w_v, wt_v):
    for y in range(OY):
        wt_v[y] = weights(w_v, y).T


def remap(pick, recv1, lhs, w_v, fscr):
    arrived = recv1[...].reshape(N_BLK * MSG, TILE)
    picked = jnp.dot(pick[...], arrived, preferred_element_type=f32).astype(bf16)
    lhs[...] = jnp.concatenate([picked[k * TILE : (k + 1) * TILE] for k in range(KSRC)], axis=1)
    for y in range(OY):
        out = jnp.dot(lhs[pl.ds(y // 2 * 16, 16), :], weights(w_v, y), preferred_element_type=f32)
        for n in range(2):
            fscr[pl.ds(n * TILE + y * 8, 8), :] = out[y % 2 * 8 : y % 2 * 8 + 8, n * TILE : (n + 1) * TILE]
    return [
        jnp.concatenate(
            [fscr[pl.ds(n * (TILE + PARTS) + p, OY, stride=8), :] for n in range(2)], axis=1
        )
        for p in range(PARTS)
    ]


def remap_back(sea, temp, push, wt_v, rscr, cscr, back, send2):
    surface = sea * (temp + push)
    ice = sea * jax.nn.sigmoid(-2.0 * (surface + 1.0))
    for f, field in enumerate((surface, ice)):
        field = field.astype(bf16).astype(f32)
        for n in range(2):
            rscr[pl.ds(n * 4 * OY + 2 * n + f, OY, stride=4), :] = field[:, n * TILE : (n + 1) * TILE]
    returned = jnp.concatenate([rscr[: 4 * OY], rscr[4 * OY :]], axis=1).astype(bf16)
    for y in range(OY):
        out = jnp.dot(returned[y // 4 * 16 : y // 4 * 16 + 16], wt_v[y], preferred_element_type=f32)
        cscr[pl.ds(y * 4, 4), :] = out[y % 4 * 4 : y % 4 * 4 + 4]
    terms = jnp.concatenate([cscr[:, k * TILE : (k + 1) * TILE] for k in range(KSRC)], axis=0)
    table = back[:, : 4 * OY * KSRC]
    top = terms.astype(bf16)
    rest = (terms - top.astype(f32)).astype(bf16)
    sums = jnp.dot(table, top, preferred_element_type=f32) + jnp.dot(table, rest, preferred_element_type=f32)
    send2[...] = sums.astype(bf16).reshape(send2.shape)


def gather_back(listed, recv2, atm_o):
    atm_o[...] = jnp.dot(listed[...], recv2[...].reshape(N_BLK * RET, TILE), preferred_element_type=f32)


def reorder(fields, table):
    rows = jnp.concatenate(fields, axis=0)
    top = rows.astype(bf16)
    rest = (rows - top.astype(f32)).astype(bf16)
    table = table[...]
    out = jnp.dot(top, table, preferred_element_type=f32) + jnp.dot(rest, table, preferred_element_type=f32)
    size = fields[0].shape[0]
    return [out[i * size : (i + 1) * size] for i in range(len(fields))]


def column_tables(spread, gather):
    lane = iota((EXT_X, TILE), 1)
    for t in range(COLUMNS):
        spread[:, t * TILE : (t + 1) * TILE] = jnp.where(
            iota((EXT_X, TILE), 0) == lane * COLUMNS + t, 1.0, 0.0
        ).astype(bf16)
    spot = iota((EXT_X, OX), 0)
    spot = spot % TILE * COLUMNS + spot // TILE
    gather[...] = jnp.where(spot == iota((EXT_X, OX), 1), 1.0, 0.0).astype(bf16)


def interleave(fields, rows, spread):
    out = []
    for i, field in enumerate(reorder(fields, spread)):
        for t in range(COLUMNS):
            rows[i, pl.ds(t * EXT_Y, EXT_Y), :] = field[:, t * TILE : (t + 1) * TILE]
        out.append(
            [
                jnp.concatenate(
                    [rows[i, pl.ds(t * EXT_Y + v, 8, stride=PLANES), :] for t in range(COLUMNS)], axis=1
                )
                for v in range(PLANES)
            ]
        )
    return out


def own_cells(fields, rows, gather):
    out = []
    for i, planes in enumerate(fields):
        for t in range(COLUMNS):
            for v in range(PLANES):
                rows[i, pl.ds(t * EXT_Y + v, 8, stride=PLANES), :] = planes[v][:, t * TILE : (t + 1) * TILE]
        out.append(jnp.concatenate([rows[i, pl.ds(t * EXT_Y, OY), :] for t in range(COLUMNS)], axis=1))
    return reorder(out, gather)


def from_east(planes):
    return [jnp.concatenate([x[:, TILE:], pltpu.roll(x[:, :TILE], TILE - 1, 1)], axis=1) for x in planes]


def from_west(planes):
    return [
        jnp.concatenate([pltpu.roll(x[:, EXT_X - TILE :], 1, 1), x[:, : EXT_X - TILE]], axis=1) for x in planes
    ]


def from_north(planes):
    return planes[1:] + [pltpu.roll(planes[0], 7, 0)]


def from_south(planes):
    return [pltpu.roll(planes[-1], 1, 0)] + planes[:-1]


def each(f, *fields):
    return [f(*planes) for planes in zip(*fields)]


CARRY = depth_step * (1.0 - drag_rate)


def start_ocean(around, rows, spread, masks, state):
    eta, east, north, sea = interleave(around, rows, spread)
    east_open = each(lambda a, b: a * b, sea, from_east(sea))
    north_open = each(lambda a, b: a * b, sea, from_north(sea))
    consts = [
        sea,
        each(lambda m: (gravity_step * depth_step) * m, east_open),
        each(lambda m: (gravity_step * depth_step) * m, north_open),
        each(lambda m: (filter_rate * (1.0 - drag_rate)) * m, east_open),
        each(lambda m: (filter_rate * (1.0 - drag_rate)) * m, north_open),
    ]
    consts += [from_west(consts[1]), from_west(consts[3])]
    east = each(lambda m, w: CARRY * m * w, east_open, east)
    north = each(lambda m, w: CARRY * m * w, north_open, north)
    for ref, fields in ((masks, consts), (state, [eta, east, from_west(east), north])):
        for i, planes in enumerate(fields):
            for v in range(PLANES):
                ref[i, v] = planes[v]


def subcycles(push, rows, spread, gather, masks, state, ocean_o):
    push = interleave(push, rows, spread)
    sea, grad_e, grad_n, keep_e, keep_n, grad_w, keep_w = (
        [masks[i, v] for v in range(PLANES)] for i in range(7)
    )
    push_e, push_n = (
        each(lambda m, f: (force_step / gravity_step) * m * f, grad, field)
        for grad, field in zip((grad_e, grad_n), push)
    )
    push_w = from_west(push_e)
    share = spread_rate / (gravity_step * depth_step)
    centre = (1.0 - 4.0 * filter_rate) / filter_rate

    def advance(_, carried):
        eta, east, west, north = (list(field) for field in carried)
        slope_e = each(lambda m, a, b: m * (a - b), grad_e, from_east(eta), eta)
        slope_w = each(lambda m, a, b: m * (a - b), grad_w, eta, from_west(eta))
        slope_n = each(lambda m, a, b: m * (a - b), grad_n, from_north(eta), eta)
        east = each(lambda w, p, a: w + p - a, east, push_e, slope_e)
        west = each(lambda w, p, a: w + p - a, west, push_w, slope_w)
        north = each(lambda w, p, a: w + p - a, north, push_n, slope_n)
        flow_n = each(lambda w, a: w - share * a, north, slope_n)
        eta = each(
            lambda m, e, a, b, x, y, c, d: m * (e - ((a - b) - share * (x - y)) - (c - d)),
            sea, eta, east, west, slope_e, slope_w, flow_n, from_south(flow_n),
        )

        def smooth(m, x, beside_e, beside_w):
            return each(
                lambda m, x, a, b, c, d: m * (centre * x + ((a + b) + (c + d))),
                m, x, beside_e, beside_w, from_north(x), from_south(x),
            )

        return (
            tuple(eta),
            tuple(smooth(keep_e, east, from_east(east), west)),
            tuple(smooth(keep_w, west, east, from_west(west))),
            tuple(smooth(keep_n, north, from_east(north), from_west(north))),
        )

    first = tuple(tuple(state[i, v] for v in range(PLANES)) for i in range(4))
    last = lax.fori_loop(0, SUBCYCLES, advance, first, unroll=True)
    last = (last[0], last[1], last[3])
    cells = own_cells(last, rows, gather)
    for i, scale in enumerate((1.0, 1.0 / CARRY, 1.0 / CARRY)):
        ocean_o[i] = scale * cells[i]


def kernel(
    state_h, temp_h, land_h, flux_h, w_h, src_h, send_h, mix_h,
    ocean_o, atm_o,
    src_s, send_s, mix_s,
    w_v, wt_v, flux_v, temp_v, land_v, own, fown,
    listing, stage, send1, recv1, send2, recv2,
    packs, fpacks, rows_in, frows_in, sides_in, fsides_in,
    idcol, pick, back, listed, lhs, fscr, rscr, cscr, rows, masks, state, spread, gather,
    load_sem, tile_send, tile_recv, back_send, back_recv,
    halo_send, halo_recv, fhalo_send, fhalo_recv,
):
    comp = lax.axis_index("comp")
    blk = lax.axis_index("blk")
    sub = lax.axis_index("sub")
    row = comp * N_SUB + sub

    def device(dx, dy):
        to_row = lax.rem(row + dy + N_ROW, N_ROW)
        return (to_row // N_SUB, lax.rem(blk + dx + N_BLK, N_BLK), lax.rem(to_row, N_SUB))

    def partner(i):
        away = N_BLK // 2 + (1 - 2 * lax.rem(i + comp, 2)) * (i // 2)
        return lax.rem(blk + away, N_BLK)

    barrier = pltpu.get_barrier_semaphore()

    def greet(i, carry):
        pl.semaphore_signal(barrier, inc=1, device_id=(comp, partner(i), sub), device_id_type=MESH)
        return carry

    lax.fori_loop(1, N_BLK, greet, 0)
    for dx, dy in ((0, 1), (0, -1), (1, 1), (1, -1), (-1, 1), (-1, -1)):
        pl.semaphore_signal(barrier, inc=1, device_id=device(dx, dy), device_id_type=MESH)

    loads = [
        pltpu.make_async_copy(src, dst, load_sem.at[i])
        for i, (src, dst) in enumerate(
            [
                (mix_h, mix_s), (flux_h, flux_v), (send_h, send_s), (src_h, src_s),
                (state_h, own.at[pl.ds(0, 3)]), (land_h, land_v), (temp_h, temp_v), (w_h, w_v),
            ]
        )
    ]
    for load in loads:
        load.start()

    for load in loads[:3]:
        load.wait()
    stage_tiles(flux_v, send_s, mix_s, listing, stage, send1)

    pl.semaphore_wait(barrier, N_BLK - 1 + 6)

    def send_all(src, dst, send_sem, recv_sem):
        def send(i, carry):
            pltpu.make_async_remote_copy(
                src_ref=src.at[partner(i)], dst_ref=dst.at[blk],
                send_sem=send_sem, recv_sem=recv_sem,
                device_id=(comp, partner(i), sub), device_id_type=MESH,
            ).start()
            return carry

        lax.fori_loop(1, N_BLK, send, 0)

    others = pl.ds(0, N_BLK - 1)

    def all_of(src, dst, sem):
        return pltpu.make_async_copy(src.at[others], dst.at[others], sem)

    send_all(send1, recv1, tile_send, tile_recv)

    def halo_copies(block, pair, rows_to, sides_to, send_sem, recv_sem):
        out = []

        def add(src, dst, dx, dy):
            i = len(out)
            out.append(
                pltpu.make_async_remote_copy(
                    src_ref=src, dst_ref=dst, send_sem=send_sem.at[i], recv_sem=recv_sem.at[i],
                    device_id=device(dx, dy), device_id_type=MESH,
                )
            )

        add(block, rows_to.at[0], 0, -1)
        add(block, rows_to.at[1], 0, 1)
        for slot, dy in ((0, 0), (1, -1), (2, 1)):
            add(pair.at[0], sides_to.at[slot], -1, dy)
            add(pair.at[1], sides_to.at[3 + slot], 1, dy)
        return out

    loads[4].wait()
    loads[5].wait()
    own[3] = land_v[...].astype(f32)
    packs[0], packs[1] = pack_sides([own[i] for i in range(4)])
    halo = halo_copies(own, packs, rows_in, sides_in, halo_send, halo_recv)
    for copy in halo:
        copy.start()
    recv1[blk] = send1[blk]

    loads[3].wait()
    tables(src_s, send_s, idcol, pick, back, listed)
    column_tables(spread, gather)
    rscr[...] = jnp.zeros_like(rscr)
    loads[6].wait()
    loads[7].wait()
    turn_weights(w_v, wt_v)

    all_of(send1, recv1, tile_recv).wait()
    forcing = remap(pick, recv1, lhs, w_v, fscr)
    fown[0], fown[1] = forcing[0], forcing[1]
    fpacks[0], fpacks[1] = pack_sides(forcing[:2])
    fhalo = halo_copies(fown, fpacks, frows_in, fsides_in, fhalo_send, fhalo_recv)
    for copy in fhalo:
        copy.start()
    remap_back(own[3], temp_v[...], forcing[2] + forcing[3], wt_v, rscr, cscr, back, send2)
    send_all(send2, recv2, back_send, back_recv)
    recv2[blk] = send2[blk]

    for copy in halo:
        copy.wait_recv()
    around = [
        extend(own[i], rows_in[0, i], rows_in[1, i], [sides_in[j] for j in range(6)], i, 4) for i in range(4)
    ]
    start_ocean(around, rows, spread, masks, state)
    for copy in fhalo:
        copy.wait_recv()
    push = [
        extend(fown[i], frows_in[0, i], frows_in[1, i], [fsides_in[j] for j in range(6)], i, 2) for i in range(2)
    ]
    subcycles(push, rows, spread, gather, masks, state, ocean_o)

    all_of(send2, recv2, back_recv).wait()
    gather_back(listed, recv2, atm_o)

    all_of(send1, recv1, tile_send).wait()
    all_of(send2, recv2, back_send).wait()
    for copy in halo + fhalo:
        copy.wait_send()


def shards(ocean_state, sea_temp, land_mask, atm_flux, remap_w, source_tile, send_tiles, flux_mix):
    hbm = pl.BlockSpec(memory_space=pltpu.HBM)
    vmem = pl.BlockSpec(memory_space=pltpu.VMEM)
    message = pltpu.VMEM((N_BLK, CAP, PARTS, TILE), bf16)
    returned = pltpu.VMEM((N_BLK, CAP, 2, TILE), bf16)
    dma = pltpu.SemaphoreType.DMA
    ocean, atm = pl.pallas_call(
        kernel,
        out_shape=(
            jax.ShapeDtypeStruct((3, OY, OX), f32),
            jax.ShapeDtypeStruct((2 * ATILES_DEV, TILE), f32),
        ),
        in_specs=[hbm] * 8,
        out_specs=(vmem, vmem),
        scratch_shapes=[
            pltpu.SMEM((KSRC, 2, OY), i32),
            pltpu.SMEM((1, CAP, 1, N_BLK), i32),
            pltpu.SMEM((3, FIELDS), f32),
            pltpu.VMEM((OY, 2, KSRC, TILE, TILE), bf16),
            pltpu.VMEM((OY, OX, KSRC * TILE), bf16),
            pltpu.VMEM((FIELDS, ATILES_DEV, TILE), bf16),
            pltpu.VMEM((OY, OX), f32),
            pltpu.VMEM((OY, OX), i32),
            pltpu.VMEM((4, OY, OX), f32),
            pltpu.VMEM((2, OY, OX), f32),
            pltpu.VMEM((N_BLK * MSG, TILE), i32),
            pltpu.VMEM((N_BLK * MSG, 4 * ATILES_DEV), bf16),
            message, message, returned, returned,
            pltpu.VMEM((2, OY, TILE), f32),
            pltpu.VMEM((2, OY, TILE), f32),
            pltpu.VMEM((2, 4, OY, OX), f32),
            pltpu.VMEM((2, 2, OY, OX), f32),
            pltpu.VMEM((6, OY, TILE), f32),
            pltpu.VMEM((6, OY, TILE), f32),
            pltpu.VMEM((ROWS, TILE), i32),
            pltpu.VMEM((ROWS, N_BLK * MSG), bf16),
            pltpu.VMEM((N_BLK * RET, 2 * TILE), bf16),
            pltpu.VMEM((2 * ATILES_DEV, N_BLK * RET), bf16),
            pltpu.VMEM((TILE, KSRC * TILE), bf16),
            pltpu.VMEM((2 * TILE, TILE), f32),
            pltpu.VMEM((8 * OY, TILE), f32),
            pltpu.VMEM((4 * OY, KSRC * TILE), f32),
            pltpu.VMEM((4, COLUMNS * EXT_Y, TILE), f32),
            pltpu.VMEM((7, PLANES, 8, EXT_X), f32),
            pltpu.VMEM((4, PLANES, 8, EXT_X), f32),
            pltpu.VMEM((EXT_X, EXT_X), bf16),
            pltpu.VMEM((EXT_X, OX), bf16),
            dma((8,)),
            dma, dma, dma, dma,
            dma((8,)), dma((8,)), dma((8,)), dma((8,)),
        ],
        compiler_params=pltpu.CompilerParams(
            collective_id=0, has_side_effects=True, vmem_limit_bytes=32 * 1024 * 1024
        ),
    )(
        *(
            pltpu.with_memory_space_constraint(x, pltpu.HBM)
            for x in (
                ocean_state, sea_temp, land_mask,
                jnp.transpose(atm_flux[0], (1, 0, 2)),
                remap_w,
                jnp.transpose(source_tile, (2, 1, 0)),
                jnp.transpose(send_tiles, (0, 3, 1, 2)),
                flux_mix,
            )
        )
    )
    return ocean, atm.reshape(1, ATILES_DEV, 2, TILE)


def solution(mesh):
    placed = (
        P(None, ("comp", "sub"), "blk"),
        P(("comp", "sub"), "blk"),
        P(("comp", "sub"), "blk"),
        P(("comp", "sub"), "blk", None, None),
        P(("comp", "sub"), "blk", None, None, None),
        P(("comp", "sub"), "blk", None),
        P(("comp", "sub"), "blk", None, None),
        P(),
    )
    return jax.shard_map(
        shards,
        mesh=mesh,
        in_specs=placed,
        out_specs=(P(None, ("comp", "sub"), "blk"), P(("comp", "sub"), "blk", None, None)),
        check_vma=False,
    )
```

```python
import functools

import jax
import jax.numpy as jnp
from jax import lax
from jax.experimental import pallas as pl
from jax.experimental.pallas import tpu as pltpu
from jax.sharding import PartitionSpec as P

MESH = pl.DeviceIdType.MESH

SUBCYCLES = 10
FIELDS = 12
TILE = 128
KSRC = 3
CAP = 3
OY = 16
OX = 256
ATILES_DEV = 64
N_BLK = 48
N_ROW = 16
N_SUB = 8

EXT_Y = 40
EXT_X = 384
PLANES = EXT_Y // 8
COLUMNS = EXT_X // TILE

PARTS = 4
MSG = CAP * PARTS
RET = CAP * 2
REFS = KSRC * OY * 2
ROWS = REFS * PARTS

drag_rate = 0.02
gravity_step = 0.6
depth_step = 0.6
force_step = 0.1
spread_rate = 0.1
filter_rate = 0.1

f32 = jnp.float32
bf16 = jnp.bfloat16
i32 = jnp.int32


def iota(shape, dim):
    return lax.broadcasted_iota(i32, shape, dim)


def pack_sides(fields):
    width = TILE // len(fields)
    lane = iota((OY, TILE), 1) // width
    first = last = jnp.zeros((OY, TILE), f32)
    for i, field in enumerate(fields):
        head, tail = field[:, :TILE], field[:, OX - TILE :]
        if i:
            head = pltpu.roll(head, i * width, 1)
        if i + 1 < len(fields):
            tail = pltpu.roll(tail, (i + 1) * width, 1)
        first = jnp.where(lane == i, head, first)
        last = jnp.where(lane == i, tail, last)
    return first, last


def extend(own, north, south, sides, i, count):
    width = TILE // count
    lane = iota((OY, TILE), 1)

    def beside(slot):
        east, west = sides[slot], sides[3 + slot]
        if i:
            east = pltpu.roll(east, TILE - i * width, 1)
        if i + 1 < count:
            west = pltpu.roll(west, TILE - (i + 1) * width, 1)
        return jnp.where(lane < TILE // 2, east, west)

    own = jnp.concatenate([own, beside(0)], axis=1)
    north = jnp.concatenate([north, beside(1)], axis=1)
    south = jnp.concatenate([south, beside(2)], axis=1)
    between = jnp.where(iota((8, EXT_X), 0) < 4, north[8:], south[:8])
    return jnp.concatenate([own, north[:8], between, south[8:]], axis=0)


def stage_tiles(flux_v, send_s, mix_s, listing, stage, send1):
    mixes = []
    for q in range(3):
        total = jnp.zeros((ATILES_DEV, TILE), f32)
        for f in range(FIELDS):
            total = total + mix_s[q, f] * flux_v[f].astype(f32)
        mixes.append(total)
    high = mixes[2].astype(bf16)
    rest = (mixes[2] - high.astype(f32)).astype(bf16)
    mixed = jnp.concatenate([mixes[0].astype(bf16), mixes[1].astype(bf16), high, rest], axis=0)

    upper = iota((8, TILE), 0) < PARTS
    for j in range(0, N_BLK, 2):
        slots = [send_s[0, s, 0, i] for i in (j, j + 1) for s in range(CAP)]
        for i in range(CAP):
            listing[pl.ds(j * MSG + i * 8, 8), :] = jnp.where(upper, slots[2 * i], slots[2 * i + 1])
    wanted = listing[...]
    part = iota((N_BLK * MSG, TILE), 0) % PARTS
    wanted = jnp.where(wanted >= 0, wanted + part * ATILES_DEV, -1)
    for c in range(2):
        stage[:, c * TILE : (c + 1) * TILE] = jnp.where(
            wanted == iota((N_BLK * MSG, TILE), 1) + c * TILE, 1.0, 0.0
        ).astype(bf16)
    rows = jnp.dot(stage[...], mixed, preferred_element_type=f32).astype(bf16)
    send1[...] = rows.reshape(send1.shape)


def tables(src_s, send_s, idcol, pick, back, listed):
    upper = iota((8, TILE), 0) < PARTS
    refs = jnp.full((1, TILE), -1, i32)
    wide = [jnp.full((1, TILE), -1, i32) for _ in range(2)]
    lane1 = iota((1, TILE), 1)
    for k in range(KSRC):
        for y in range(OY):
            both = [src_s[k, n, y] for n in range(2)]
            idcol[pl.ds((k * OY + y) * 8, 8), :] = jnp.where(upper, both[0], both[1])
            for n, value in enumerate(both):
                place = (k * OY + y) * 2 + n
                refs = jnp.where(lane1 == place, value, refs)
                wide[place // 64] = jnp.where(lane1 // 2 == place % 64, value, wide[place // 64])
    ids = idcol[...]
    spot = iota((ROWS, TILE), 0) // PARTS
    part = iota((ROWS, TILE), 0) % PARTS
    at = iota((ROWS, TILE), 1)
    again = jnp.max(jnp.where((ids == refs) & (spot < at), 1, 0), axis=0, keepdims=True)
    owners = ids // ATILES_DEV
    lower = (refs // ATILES_DEV == owners) & (refs < ids) & (again == 0) & (refs >= 0)
    rank = jnp.dot(
        jnp.where(lower, 1.0, 0.0).astype(bf16), jnp.ones((TILE, TILE), bf16), preferred_element_type=f32
    ).astype(i32)
    target = owners * MSG + rank * PARTS + part
    for c in range(0, N_BLK * MSG, TILE):
        width = min(TILE, N_BLK * MSG - c)
        pick[:, c : c + width] = jnp.where(target == at + c, 1.0, 0.0).astype(bf16)[:, :width]
    first = jnp.where(part == 0, rank, 0)
    for c in range(2):
        rank_line = jnp.sum(jnp.where(spot == at // 2 + c * 64, first, 0), axis=0, keepdims=True)
        to = (wide[c] // ATILES_DEV) * RET + rank_line * 2 + lane1 % 2
        to = jnp.where(wide[c] >= 0, to, -1)
        back[:, c * TILE : (c + 1) * TILE] = jnp.where(to == iota((N_BLK * RET, TILE), 0), 1.0, 0.0).astype(bf16)
    slot = [jnp.full((1, TILE), -1, i32) for _ in range(3)]
    for j in range(N_BLK):
        for s in range(CAP):
            place = j * CAP + s
            slot[place // 64] = jnp.where(lane1 // 2 == place % 64, send_s[0, s, 0, j], slot[place // 64])
    for c in range(3):
        width = min(TILE, N_BLK * RET - c * TILE)
        hit = slot[c] * 2 + lane1 % 2 == iota((2 * ATILES_DEV, TILE), 0)
        listed[:, c * TILE : c * TILE + width] = jnp.where(hit, 1.0, 0.0).astype(bf16)[:, :width]


def weights(w_v, y):
    return jnp.concatenate([w_v[y, n].reshape(KSRC * TILE, TILE) for n in range(2)], axis=1)


def turn_weights(w_v, wt_v):
    for y in range(0, OY, 2):
        for i in range(2):
            wt_v[y // 2, :, i * KSRC * TILE : (i + 1) * KSRC * TILE] = weights(w_v, y + i).T


def remap(pick, recv1, lhs, w_v, fscr):
    arrived = recv1[...].reshape(N_BLK * MSG, TILE)
    picked = jnp.dot(pick[...], arrived, preferred_element_type=f32).astype(bf16)
    lhs[...] = jnp.concatenate([picked[k * TILE : (k + 1) * TILE] for k in range(KSRC)], axis=1)
    upper = iota((16, KSRC * TILE), 0) < 8
    for y in range(0, OY, 2):
        both = lhs[pl.ds(y * 8, 16), :]
        halves = [jnp.where(upper, both, 0), jnp.where(upper, 0, both)]
        out = jnp.dot(
            jnp.concatenate(halves, axis=1), jnp.concatenate([weights(w_v, y), weights(w_v, y + 1)], axis=0),
            preferred_element_type=f32,
        )
        for n in range(2):
            fscr[pl.ds(n * TILE + y * 8, 16), :] = out[:, n * TILE : (n + 1) * TILE]
    return [
        jnp.concatenate(
            [fscr[pl.ds(n * (TILE + PARTS) + p, OY, stride=8), :] for n in range(2)], axis=1
        )
        for p in range(PARTS)
    ]


def remap_back(sea, temp, push, wt_v, rscr, cscr, back, send2):
    surface = sea * (temp + push)
    ice = sea * jax.nn.sigmoid(-2.0 * (surface + 1.0))
    for f, field in enumerate((surface, ice)):
        field = field.astype(bf16).astype(f32)
        for n in range(2):
            rscr[pl.ds(n * 4 * OY + 2 * n + f, OY, stride=4), :] = field[:, n * TILE : (n + 1) * TILE]
    returned = jnp.concatenate([rscr[: 4 * OY], rscr[4 * OY :]], axis=1).astype(bf16)
    for y in range(0, OY, 2):
        out = jnp.dot(returned[y // 4 * 16 : y // 4 * 16 + 16], wt_v[y // 2], preferred_element_type=f32)
        for i in range(2):
            start = (y + i) % 4 * 4
            cscr[pl.ds((y + i) * 4, 4), :] = out[start : start + 4, i * KSRC * TILE : (i + 1) * KSRC * TILE]
    terms = jnp.concatenate([cscr[:, k * TILE : (k + 1) * TILE] for k in range(KSRC)], axis=0)
    table = back[:, : 4 * OY * KSRC]
    top = terms.astype(bf16)
    rest = (terms - top.astype(f32)).astype(bf16)
    sums = jnp.dot(table, top, preferred_element_type=f32) + jnp.dot(table, rest, preferred_element_type=f32)
    send2[...] = sums.astype(bf16).reshape(send2.shape)


def gather_back(listed, recv2, atm_o):
    atm_o[...] = jnp.dot(listed[...], recv2[...].reshape(N_BLK * RET, TILE), preferred_element_type=f32)


def reorder(fields, table):
    rows = jnp.concatenate(fields, axis=0)
    top = rows.astype(bf16)
    rest = (rows - top.astype(f32)).astype(bf16)
    table = table[...]
    out = jnp.dot(top, table, preferred_element_type=f32) + jnp.dot(rest, table, preferred_element_type=f32)
    size = fields[0].shape[0]
    return [out[i * size : (i + 1) * size] for i in range(len(fields))]


def column_tables(spread, gather):
    lane = iota((EXT_X, TILE), 1)
    for t in range(COLUMNS):
        spread[:, t * TILE : (t + 1) * TILE] = jnp.where(
            iota((EXT_X, TILE), 0) == lane * COLUMNS + t, 1.0, 0.0
        ).astype(bf16)
    spot = iota((EXT_X, OX), 0)
    spot = spot % TILE * COLUMNS + spot // TILE
    gather[...] = jnp.where(spot == iota((EXT_X, OX), 1), 1.0, 0.0).astype(bf16)


def interleave(fields, rows, spread):
    out = []
    for i, field in enumerate(reorder(fields, spread)):
        for t in range(COLUMNS):
            rows[i, pl.ds(t * EXT_Y, EXT_Y), :] = field[:, t * TILE : (t + 1) * TILE]
        out.append(
            [
                jnp.concatenate(
                    [rows[i, pl.ds(t * EXT_Y + v, 8, stride=PLANES), :] for t in range(COLUMNS)], axis=1
                )
                for v in range(PLANES)
            ]
        )
    return out


def own_cells(fields, rows, gather):
    out = []
    for i, planes in enumerate(fields):
        for t in range(COLUMNS):
            for v in range(PLANES):
                rows[i, pl.ds(t * EXT_Y + v, 8, stride=PLANES), :] = planes[v][:, t * TILE : (t + 1) * TILE]
        out.append(jnp.concatenate([rows[i, pl.ds(t * EXT_Y, OY), :] for t in range(COLUMNS)], axis=1))
    return reorder(out, gather)


def from_east(planes):
    return [jnp.concatenate([x[:, TILE:], pltpu.roll(x[:, :TILE], TILE - 1, 1)], axis=1) for x in planes]


def from_west(planes):
    return [
        jnp.concatenate([pltpu.roll(x[:, EXT_X - TILE :], 1, 1), x[:, : EXT_X - TILE]], axis=1) for x in planes
    ]


def from_north(planes):
    return planes[1:] + [pltpu.roll(planes[0], 7, 0)]


def from_south(planes):
    return [pltpu.roll(planes[-1], 1, 0)] + planes[:-1]


def each(f, *fields):
    return [f(*planes) for planes in zip(*fields)]


CARRY = depth_step * (1.0 - drag_rate)


def start_ocean(around, rows, spread, masks, state):
    eta, east, north, sea = interleave(around, rows, spread)
    east_open = each(lambda a, b: a * b, sea, from_east(sea))
    north_open = each(lambda a, b: a * b, sea, from_north(sea))
    consts = [
        sea,
        each(lambda m: (gravity_step * depth_step) * m, east_open),
        each(lambda m: (gravity_step * depth_step) * m, north_open),
        each(lambda m: (filter_rate * (1.0 - drag_rate)) * m, east_open),
        each(lambda m: (filter_rate * (1.0 - drag_rate)) * m, north_open),
    ]
    consts += [from_west(consts[1]), from_west(consts[3])]
    east = each(lambda m, w: CARRY * m * w, east_open, east)
    north = each(lambda m, w: CARRY * m * w, north_open, north)
    for ref, fields in ((masks, consts), (state, [eta, east, from_west(east), north])):
        for i, planes in enumerate(fields):
            for v in range(PLANES):
                ref[i, v] = planes[v]


def subcycles(push, rows, spread, gather, masks, state, ocean_o):
    push = interleave(push, rows, spread)
    sea, grad_e, grad_n, keep_e, keep_n, grad_w, keep_w = (
        [masks[i, v] for v in range(PLANES)] for i in range(7)
    )
    push_e, push_n = (
        each(lambda m, f: (force_step / gravity_step) * m * f, grad, field)
        for grad, field in zip((grad_e, grad_n), push)
    )
    push_w = from_west(push_e)
    share = spread_rate / (gravity_step * depth_step)
    centre = (1.0 - 4.0 * filter_rate) / filter_rate

    def advance(_, carried):
        eta, east, west, north = (list(field) for field in carried)
        slope_e = each(lambda m, a, b: m * (a - b), grad_e, from_east(eta), eta)
        slope_w = each(lambda m, a, b: m * (a - b), grad_w, eta, from_west(eta))
        slope_n = each(lambda m, a, b: m * (a - b), grad_n, from_north(eta), eta)
        east = each(lambda w, p, a: w + p - a, east, push_e, slope_e)
        west = each(lambda w, p, a: w + p - a, west, push_w, slope_w)
        north = each(lambda w, p, a: w + p - a, north, push_n, slope_n)
        flow_n = each(lambda w, a: w - share * a, north, slope_n)
        eta = each(
            lambda m, e, a, b, x, y, c, d: m * (e - ((a - b) - share * (x - y)) - (c - d)),
            sea, eta, east, west, slope_e, slope_w, flow_n, from_south(flow_n),
        )

        def smooth(m, x, beside_e, beside_w):
            return each(
                lambda m, x, a, b, c, d: m * (centre * x + ((a + b) + (c + d))),
                m, x, beside_e, beside_w, from_north(x), from_south(x),
            )

        return (
            tuple(eta),
            tuple(smooth(keep_e, east, from_east(east), west)),
            tuple(smooth(keep_w, west, east, from_west(west))),
            tuple(smooth(keep_n, north, from_east(north), from_west(north))),
        )

    first = tuple(tuple(state[i, v] for v in range(PLANES)) for i in range(4))
    last = lax.fori_loop(0, SUBCYCLES, advance, first, unroll=True)
    last = (last[0], last[1], last[3])
    cells = own_cells(last, rows, gather)
    for i, scale in enumerate((1.0, 1.0 / CARRY, 1.0 / CARRY)):
        ocean_o[i] = scale * cells[i]


def kernel(
    state_h, temp_h, land_h, flux_h, w_h, src_h, send_h, mix_h,
    ocean_o, atm_o,
    src_s, send_s, mix_s,
    w_v, wt_v, flux_v, temp_v, land_v, own, fown,
    listing, stage, send1, recv1, send2, recv2,
    packs, fpacks, rows_in, frows_in, sides_in, fsides_in,
    idcol, pick, back, listed, lhs, fscr, rscr, cscr, rows, masks, state, spread, gather,
    load_sem, tile_send, tile_recv, back_send, back_recv,
    halo_send, halo_recv, fhalo_send, fhalo_recv, ready,
):
    comp = lax.axis_index("comp")
    blk = lax.axis_index("blk")
    sub = lax.axis_index("sub")
    row = comp * N_SUB + sub

    def device(dx, dy):
        to_row = lax.rem(row + dy + N_ROW, N_ROW)
        return (to_row // N_SUB, lax.rem(blk + dx + N_BLK, N_BLK), lax.rem(to_row, N_SUB))

    def partner(i):
        away = N_BLK // 2 + (1 - 2 * lax.rem(i + comp, 2)) * (i // 2)
        return lax.rem(blk + away, N_BLK)

    barrier = pltpu.get_barrier_semaphore()

    def greet(i, carry):
        pl.semaphore_signal(barrier, inc=1, device_id=(comp, partner(i), sub), device_id_type=MESH)
        return carry

    lax.fori_loop(1, N_BLK, greet, 0)
    for dy in (1, -1):
        pl.semaphore_signal(barrier, inc=1, device_id=device(0, dy), device_id_type=MESH)

    loads = [
        pltpu.make_async_copy(src, dst, load_sem.at[i])
        for i, (src, dst) in enumerate(
            [
                (mix_h, mix_s), (flux_h, flux_v), (send_h, send_s), (src_h, src_s),
                (state_h, own.at[pl.ds(0, 3)]), (land_h, land_v), (temp_h, temp_v), (w_h, w_v),
            ]
        )
    ]
    for load in loads:
        load.start()

    for load in loads[:3]:
        load.wait()
    stage_tiles(flux_v, send_s, mix_s, listing, stage, send1)

    pl.semaphore_wait(barrier, N_BLK - 1 + 2)
    for dy in (1, -1):
        pl.semaphore_signal(ready, inc=1, device_id=device(0, dy), device_id_type=MESH)

    def send_all(src, dst, send_sem, recv_sem):
        def send(i, carry):
            pltpu.make_async_remote_copy(
                src_ref=src.at[partner(i)], dst_ref=dst.at[blk],
                send_sem=send_sem, recv_sem=recv_sem,
                device_id=(comp, partner(i), sub), device_id_type=MESH,
            ).start()
            return carry

        lax.fori_loop(1, N_BLK, send, 0)

    others = pl.ds(0, N_BLK - 1)

    def all_of(src, dst, sem):
        return pltpu.make_async_copy(src.at[others], dst.at[others], sem)

    send_all(send1, recv1, tile_send, tile_recv)

    def halo_copies(block, pair, rows_to, sides_to, send_sem, recv_sem):
        out = []

        def add(src, dst, dx, dy):
            i = len(out)
            out.append(
                pltpu.make_async_remote_copy(
                    src_ref=src, dst_ref=dst, send_sem=send_sem.at[i], recv_sem=recv_sem.at[i],
                    device_id=device(dx, dy), device_id_type=MESH,
                )
            )

        add(block, rows_to.at[0], 0, -1)
        add(block, rows_to.at[1], 0, 1)
        for slot, dy in ((0, 0), (1, -1), (2, 1)):
            add(pair.at[0], sides_to.at[slot], -1, dy)
            add(pair.at[1], sides_to.at[3 + slot], 1, dy)
        return out

    loads[4].wait()
    loads[5].wait()
    own[3] = land_v[...].astype(f32)
    packs[0], packs[1] = pack_sides([own[i] for i in range(4)])
    recv1[blk] = send1[blk]

    loads[3].wait()
    tables(src_s, send_s, idcol, pick, back, listed)
    column_tables(spread, gather)
    rscr[...] = jnp.zeros_like(rscr)
    loads[6].wait()
    loads[7].wait()
    turn_weights(w_v, wt_v)
    pl.semaphore_wait(ready, 2)
    halo = halo_copies(own, packs, rows_in, sides_in, halo_send, halo_recv)
    for copy in halo:
        copy.start()

    all_of(send1, recv1, tile_recv).wait()
    forcing = remap(pick, recv1, lhs, w_v, fscr)
    fown[0], fown[1] = forcing[0], forcing[1]
    fpacks[0], fpacks[1] = pack_sides(forcing[:2])
    fhalo = halo_copies(fown, fpacks, frows_in, fsides_in, fhalo_send, fhalo_recv)
    for copy in fhalo:
        copy.start()
    remap_back(own[3], temp_v[...], forcing[2] + forcing[3], wt_v, rscr, cscr, back, send2)
    send_all(send2, recv2, back_send, back_recv)
    recv2[blk] = send2[blk]

    for copy in halo:
        copy.wait_recv()
    around = [
        extend(own[i], rows_in[0, i], rows_in[1, i], [sides_in[j] for j in range(6)], i, 4) for i in range(4)
    ]
    start_ocean(around, rows, spread, masks, state)
    for copy in fhalo:
        copy.wait_recv()
    push = [
        extend(fown[i], frows_in[0, i], frows_in[1, i], [fsides_in[j] for j in range(6)], i, 2) for i in range(2)
    ]
    subcycles(push, rows, spread, gather, masks, state, ocean_o)

    all_of(send2, recv2, back_recv).wait()
    gather_back(listed, recv2, atm_o)

    all_of(send1, recv1, tile_send).wait()
    all_of(send2, recv2, back_send).wait()
    for copy in halo + fhalo:
        copy.wait_send()


def shards(ocean_state, sea_temp, land_mask, atm_flux, remap_w, source_tile, send_tiles, flux_mix):
    hbm = pl.BlockSpec(memory_space=pltpu.HBM)
    vmem = pl.BlockSpec(memory_space=pltpu.VMEM)
    message = pltpu.VMEM((N_BLK, CAP, PARTS, TILE), bf16)
    returned = pltpu.VMEM((N_BLK, CAP, 2, TILE), bf16)
    dma = pltpu.SemaphoreType.DMA
    ocean, atm = pl.pallas_call(
        kernel,
        out_shape=(
            jax.ShapeDtypeStruct((3, OY, OX), f32),
            jax.ShapeDtypeStruct((2 * ATILES_DEV, TILE), f32),
        ),
        in_specs=[hbm] * 8,
        out_specs=(vmem, vmem),
        scratch_shapes=[
            pltpu.SMEM((KSRC, 2, OY), i32),
            pltpu.SMEM((1, CAP, 1, N_BLK), i32),
            pltpu.SMEM((3, FIELDS), f32),
            pltpu.VMEM((OY, 2, KSRC, TILE, TILE), bf16),
            pltpu.VMEM((OY // 2, OX, 2 * KSRC * TILE), bf16),
            pltpu.VMEM((FIELDS, ATILES_DEV, TILE), bf16),
            pltpu.VMEM((OY, OX), f32),
            pltpu.VMEM((OY, OX), i32),
            pltpu.VMEM((4, OY, OX), f32),
            pltpu.VMEM((2, OY, OX), f32),
            pltpu.VMEM((N_BLK * MSG, TILE), i32),
            pltpu.VMEM((N_BLK * MSG, 4 * ATILES_DEV), bf16),
            message, message, returned, returned,
            pltpu.VMEM((2, OY, TILE), f32),
            pltpu.VMEM((2, OY, TILE), f32),
            pltpu.VMEM((2, 4, OY, OX), f32),
            pltpu.VMEM((2, 2, OY, OX), f32),
            pltpu.VMEM((6, OY, TILE), f32),
            pltpu.VMEM((6, OY, TILE), f32),
            pltpu.VMEM((ROWS, TILE), i32),
            pltpu.VMEM((ROWS, N_BLK * MSG), bf16),
            pltpu.VMEM((N_BLK * RET, 2 * TILE), bf16),
            pltpu.VMEM((2 * ATILES_DEV, N_BLK * RET), bf16),
            pltpu.VMEM((TILE, KSRC * TILE), bf16),
            pltpu.VMEM((2 * TILE, TILE), f32),
            pltpu.VMEM((8 * OY, TILE), f32),
            pltpu.VMEM((4 * OY, KSRC * TILE), f32),
            pltpu.VMEM((4, COLUMNS * EXT_Y, TILE), f32),
            pltpu.VMEM((7, PLANES, 8, EXT_X), f32),
            pltpu.VMEM((4, PLANES, 8, EXT_X), f32),
            pltpu.VMEM((EXT_X, EXT_X), bf16),
            pltpu.VMEM((EXT_X, OX), bf16),
            dma((8,)),
            dma, dma, dma, dma,
            dma((8,)), dma((8,)), dma((8,)), dma((8,)),
            pltpu.SemaphoreType.REGULAR,
        ],
        compiler_params=pltpu.CompilerParams(
            collective_id=0, has_side_effects=True, vmem_limit_bytes=32 * 1024 * 1024
        ),
    )(
        *(
            pltpu.with_memory_space_constraint(x, pltpu.HBM)
            for x in (
                ocean_state, sea_temp, land_mask,
                jnp.transpose(atm_flux[0], (1, 0, 2)),
                remap_w,
                jnp.transpose(source_tile, (2, 1, 0)),
                jnp.transpose(send_tiles, (0, 3, 1, 2)),
                flux_mix,
            )
        )
    )
    return ocean, atm.reshape(1, ATILES_DEV, 2, TILE)


def solution(mesh):
    placed = (
        P(None, ("comp", "sub"), "blk"),
        P(("comp", "sub"), "blk"),
        P(("comp", "sub"), "blk"),
        P(("comp", "sub"), "blk", None, None),
        P(("comp", "sub"), "blk", None, None, None),
        P(("comp", "sub"), "blk", None),
        P(("comp", "sub"), "blk", None, None),
        P(),
    )
    return jax.shard_map(
        shards,
        mesh=mesh,
        in_specs=placed,
        out_specs=(P(None, ("comp", "sub"), "blk"), P(("comp", "sub"), "blk", None, None)),
        check_vma=False,
    )
```

```python
import functools

import jax
import jax.numpy as jnp
from jax import lax
from jax.experimental import pallas as pl
from jax.experimental.pallas import tpu as pltpu
from jax.sharding import PartitionSpec as P

MESH = pl.DeviceIdType.MESH

SUBCYCLES = 10
FIELDS = 12
TILE = 128
KSRC = 3
CAP = 3
OY = 16
OX = 256
ATILES_DEV = 64
N_BLK = 48
N_ROW = 16
N_SUB = 8

EXT_Y = 40
EXT_X = 384
PLANES = EXT_Y // 8
COLUMNS = EXT_X // TILE

PARTS = 4
MSG = CAP * PARTS
RET = CAP * 2
REFS = KSRC * OY * 2
ROWS = REFS * PARTS

drag_rate = 0.02
gravity_step = 0.6
depth_step = 0.6
force_step = 0.1
spread_rate = 0.1
filter_rate = 0.1

f32 = jnp.float32
bf16 = jnp.bfloat16
i32 = jnp.int32


def iota(shape, dim):
    return lax.broadcasted_iota(i32, shape, dim)


def pack_sides(fields):
    width = TILE // len(fields)
    lane = iota((OY, TILE), 1) // width
    first = last = jnp.zeros((OY, TILE), f32)
    for i, field in enumerate(fields):
        head, tail = field[:, :TILE], field[:, OX - TILE :]
        if i:
            head = pltpu.roll(head, i * width, 1)
        if i + 1 < len(fields):
            tail = pltpu.roll(tail, (i + 1) * width, 1)
        first = jnp.where(lane == i, head, first)
        last = jnp.where(lane == i, tail, last)
    return first, last


def extend(own, north, south, sides, i, count):
    width = TILE // count
    lane = iota((OY, TILE), 1)

    def beside(slot):
        east, west = sides[slot], sides[3 + slot]
        if i:
            east = pltpu.roll(east, TILE - i * width, 1)
        if i + 1 < count:
            west = pltpu.roll(west, TILE - (i + 1) * width, 1)
        return jnp.where(lane < TILE // 2, east, west)

    own = jnp.concatenate([own, beside(0)], axis=1)
    north = jnp.concatenate([north, beside(1)], axis=1)
    south = jnp.concatenate([south, beside(2)], axis=1)
    between = jnp.where(iota((8, EXT_X), 0) < 4, north[8:], south[:8])
    return jnp.concatenate([own, north[:8], between, south[8:]], axis=0)


def stage_tiles(flux_v, send_s, mix_s, listing, stage, send1):
    mixes = []
    for q in range(3):
        total = jnp.zeros((ATILES_DEV, TILE), f32)
        for f in range(FIELDS):
            total = total + mix_s[q, f] * flux_v[f].astype(f32)
        mixes.append(total)
    high = mixes[2].astype(bf16)
    rest = (mixes[2] - high.astype(f32)).astype(bf16)
    mixed = jnp.concatenate([mixes[0].astype(bf16), mixes[1].astype(bf16), high, rest], axis=0)

    upper = iota((8, TILE), 0) < PARTS
    for j in range(0, N_BLK, 2):
        slots = [send_s[0, s, 0, i] for i in (j, j + 1) for s in range(CAP)]
        for i in range(CAP):
            listing[pl.ds(j * MSG + i * 8, 8), :] = jnp.where(upper, slots[2 * i], slots[2 * i + 1])
    wanted = listing[...]
    part = iota((N_BLK * MSG, TILE), 0) % PARTS
    wanted = jnp.where(wanted >= 0, wanted + part * ATILES_DEV, -1)
    for c in range(2):
        stage[:, c * TILE : (c + 1) * TILE] = jnp.where(
            wanted == iota((N_BLK * MSG, TILE), 1) + c * TILE, 1.0, 0.0
        ).astype(bf16)
    rows = jnp.dot(stage[...], mixed, preferred_element_type=f32).astype(bf16)
    send1[...] = rows.reshape(send1.shape)


def tables(src_s, send_s, idcol, pick, back, listed):
    upper = iota((8, TILE), 0) < PARTS
    refs = jnp.full((1, TILE), -1, i32)
    wide = [jnp.full((1, TILE), -1, i32) for _ in range(2)]
    lane1 = iota((1, TILE), 1)
    for k in range(KSRC):
        for y in range(OY):
            both = [src_s[k, n, y] for n in range(2)]
            idcol[pl.ds((k * OY + y) * 8, 8), :] = jnp.where(upper, both[0], both[1])
            for n, value in enumerate(both):
                place = (k * OY + y) * 2 + n
                refs = jnp.where(lane1 == place, value, refs)
                wide[place // 64] = jnp.where(lane1 // 2 == place % 64, value, wide[place // 64])
    ids = idcol[...]
    spot = iota((ROWS, TILE), 0) // PARTS
    part = iota((ROWS, TILE), 0) % PARTS
    at = iota((ROWS, TILE), 1)
    again = jnp.max(jnp.where((ids == refs) & (spot < at), 1, 0), axis=0, keepdims=True)
    owners = ids // ATILES_DEV
    lower = (refs // ATILES_DEV == owners) & (refs < ids) & (again == 0) & (refs >= 0)
    rank = jnp.dot(
        jnp.where(lower, 1.0, 0.0).astype(bf16), jnp.ones((TILE, TILE), bf16), preferred_element_type=f32
    ).astype(i32)
    target = owners * MSG + rank * PARTS + part
    for c in range(0, N_BLK * MSG, TILE):
        width = min(TILE, N_BLK * MSG - c)
        pick[:, c : c + width] = jnp.where(target == at + c, 1.0, 0.0).astype(bf16)[:, :width]
    first = jnp.where(part == 0, rank, 0)
    for c in range(2):
        rank_line = jnp.sum(jnp.where(spot == at // 2 + c * 64, first, 0), axis=0, keepdims=True)
        to = (wide[c] // ATILES_DEV) * RET + rank_line * 2 + lane1 % 2
        to = jnp.where(wide[c] >= 0, to, -1)
        back[:, c * TILE : (c + 1) * TILE] = jnp.where(to == iota((N_BLK * RET, TILE), 0), 1.0, 0.0).astype(bf16)
    slot = [jnp.full((1, TILE), -1, i32) for _ in range(3)]
    for j in range(N_BLK):
        for s in range(CAP):
            place = j * CAP + s
            slot[place // 64] = jnp.where(lane1 // 2 == place % 64, send_s[0, s, 0, j], slot[place // 64])
    for c in range(3):
        width = min(TILE, N_BLK * RET - c * TILE)
        hit = slot[c] * 2 + lane1 % 2 == iota((2 * ATILES_DEV, TILE), 0)
        listed[:, c * TILE : c * TILE + width] = jnp.where(hit, 1.0, 0.0).astype(bf16)[:, :width]


def weights(w_v, y):
    return jnp.concatenate([w_v[y, n].reshape(KSRC * TILE, TILE) for n in range(2)], axis=1)


def turn_weights(w_v, wt_v):
    for y in range(0, OY, 2):
        for i in range(2):
            wt_v[y // 2, :, i * KSRC * TILE : (i + 1) * KSRC * TILE] = weights(w_v, y + i).T


def remap(pick, recv1, lhs, w_v, fscr):
    arrived = recv1[...].reshape(N_BLK * MSG, TILE)
    picked = jnp.dot(pick[...], arrived, preferred_element_type=f32).astype(bf16)
    lhs[...] = jnp.concatenate([picked[k * TILE : (k + 1) * TILE] for k in range(KSRC)], axis=1)
    upper = iota((16, KSRC * TILE), 0) < 8
    for y in range(0, OY, 2):
        both = lhs[pl.ds(y * 8, 16), :]
        halves = [jnp.where(upper, both, 0), jnp.where(upper, 0, both)]
        out = jnp.dot(
            jnp.concatenate(halves, axis=1), jnp.concatenate([weights(w_v, y), weights(w_v, y + 1)], axis=0),
            preferred_element_type=f32,
        )
        for n in range(2):
            fscr[pl.ds(n * TILE + y * 8, 16), :] = out[:, n * TILE : (n + 1) * TILE]
    return [
        jnp.concatenate(
            [fscr[pl.ds(n * (TILE + PARTS) + p, OY, stride=8), :] for n in range(2)], axis=1
        )
        for p in range(PARTS)
    ]


def remap_back(sea, temp, push, wt_v, rscr, cscr, back, send2):
    surface = sea * (temp + push)
    ice = sea * jax.nn.sigmoid(-2.0 * (surface + 1.0))
    for f, field in enumerate((surface, ice)):
        field = field.astype(bf16).astype(f32)
        for n in range(2):
            rscr[pl.ds(n * 4 * OY + 2 * n + f, OY, stride=4), :] = field[:, n * TILE : (n + 1) * TILE]
    returned = jnp.concatenate([rscr[: 4 * OY], rscr[4 * OY : 8 * OY]], axis=1).astype(bf16)
    for y in range(0, OY, 2):
        out = jnp.dot(returned[y // 4 * 16 : y // 4 * 16 + 16], wt_v[y // 2], preferred_element_type=f32)
        for i in range(2):
            start = (y + i) % 4 * 4
            cscr[pl.ds((y + i) * 4, 4), :] = out[start : start + 4, i * KSRC * TILE : (i + 1) * KSRC * TILE]
    terms = jnp.concatenate([cscr[:, k * TILE : (k + 1) * TILE] for k in range(KSRC)], axis=0)
    table = back[:, : 4 * OY * KSRC]
    top = terms.astype(bf16)
    rest = (terms - top.astype(f32)).astype(bf16)
    sums = jnp.dot(table, top, preferred_element_type=f32) + jnp.dot(table, rest, preferred_element_type=f32)
    send2[...] = sums.astype(bf16).reshape(send2.shape)


def gather_back(listed, recv2, atm_o):
    atm_o[...] = jnp.dot(listed[...], recv2[...].reshape(N_BLK * RET, TILE), preferred_element_type=f32)


def reorder(fields, table):
    rows = jnp.concatenate(fields, axis=0)
    top = rows.astype(bf16)
    rest = (rows - top.astype(f32)).astype(bf16)
    out = jnp.dot(
        jnp.concatenate([top, rest], axis=1), jnp.concatenate([table[...]] * 2, axis=0), preferred_element_type=f32
    )
    size = fields[0].shape[0]
    return [out[i * size : (i + 1) * size] for i in range(len(fields))]


def column_tables(spread, gather):
    lane = iota((EXT_X, TILE), 1)
    for t in range(COLUMNS):
        spread[:, t * TILE : (t + 1) * TILE] = jnp.where(
            iota((EXT_X, TILE), 0) == lane * COLUMNS + t, 1.0, 0.0
        ).astype(bf16)
    spot = iota((EXT_X, OX), 0)
    spot = spot % TILE * COLUMNS + spot // TILE
    gather[...] = jnp.where(spot == iota((EXT_X, OX), 1), 1.0, 0.0).astype(bf16)


def interleave(fields, rows, spread):
    out = []
    for i, field in enumerate(reorder(fields, spread)):
        for t in range(COLUMNS):
            rows[i, pl.ds(t * EXT_Y, EXT_Y), :] = field[:, t * TILE : (t + 1) * TILE]
        out.append(
            [
                jnp.concatenate(
                    [rows[i, pl.ds(t * EXT_Y + v, 8, stride=PLANES), :] for t in range(COLUMNS)], axis=1
                )
                for v in range(PLANES)
            ]
        )
    return out


def own_cells(fields, rows, gather):
    out = []
    for i, planes in enumerate(fields):
        for t in range(COLUMNS):
            for v in range(PLANES):
                rows[i, pl.ds(t * EXT_Y + v, 8, stride=PLANES), :] = planes[v][:, t * TILE : (t + 1) * TILE]
        out.append(jnp.concatenate([rows[i, pl.ds(t * EXT_Y, OY), :] for t in range(COLUMNS)], axis=1))
    return reorder(out, gather)


def from_east(planes):
    return [jnp.concatenate([x[:, TILE:], pltpu.roll(x[:, :TILE], TILE - 1, 1)], axis=1) for x in planes]


def from_west(planes):
    return [
        jnp.concatenate([pltpu.roll(x[:, EXT_X - TILE :], 1, 1), x[:, : EXT_X - TILE]], axis=1) for x in planes
    ]


def from_north(planes):
    return planes[1:] + [pltpu.roll(planes[0], 7, 0)]


def from_south(planes):
    return [pltpu.roll(planes[-1], 1, 0)] + planes[:-1]


def each(f, *fields):
    return [f(*planes) for planes in zip(*fields)]


CARRY = depth_step * (1.0 - drag_rate)


def start_ocean(around, rows, spread, masks, state):
    eta, east, north, sea = interleave(around, rows, spread)
    east_open = each(lambda a, b: a * b, sea, from_east(sea))
    north_open = each(lambda a, b: a * b, sea, from_north(sea))
    consts = [
        sea,
        each(lambda m: (gravity_step * depth_step) * m, east_open),
        each(lambda m: (gravity_step * depth_step) * m, north_open),
        each(lambda m: (filter_rate * (1.0 - drag_rate)) * m, east_open),
        each(lambda m: (filter_rate * (1.0 - drag_rate)) * m, north_open),
    ]
    consts += [from_west(consts[1]), from_west(consts[3])]
    east = each(lambda m, w: CARRY * m * w, east_open, east)
    north = each(lambda m, w: CARRY * m * w, north_open, north)
    for ref, fields in ((masks, consts), (state, [eta, east, from_west(east), north])):
        for i, planes in enumerate(fields):
            for v in range(PLANES):
                ref[i, v] = planes[v]


def subcycles(push, rows, spread, masks, state):
    push = interleave(push, rows, spread)
    sea, grad_e, grad_n, keep_e, keep_n, grad_w, keep_w = (
        [masks[i, v] for v in range(PLANES)] for i in range(7)
    )
    push_e, push_n = (
        each(lambda m, f: (force_step / gravity_step) * m * f, grad, field)
        for grad, field in zip((grad_e, grad_n), push)
    )
    push_w = from_west(push_e)
    share = spread_rate / (gravity_step * depth_step)
    centre = (1.0 - 4.0 * filter_rate) / filter_rate

    def advance(_, carried):
        eta, east, west, north = (list(field) for field in carried)
        slope_e = each(lambda m, a, b: m * (a - b), grad_e, from_east(eta), eta)
        slope_w = each(lambda m, a, b: m * (a - b), grad_w, eta, from_west(eta))
        slope_n = each(lambda m, a, b: m * (a - b), grad_n, from_north(eta), eta)
        east = each(lambda w, p, a: w + p - a, east, push_e, slope_e)
        west = each(lambda w, p, a: w + p - a, west, push_w, slope_w)
        north = each(lambda w, p, a: w + p - a, north, push_n, slope_n)
        flow_n = each(lambda w, a: w - share * a, north, slope_n)
        eta = each(
            lambda m, e, a, b, x, y, c, d: m * (e - ((a - b) - share * (x - y)) - (c - d)),
            sea, eta, east, west, slope_e, slope_w, flow_n, from_south(flow_n),
        )

        def smooth(m, x, beside_e, beside_w):
            return each(
                lambda m, x, a, b, c, d: m * (centre * x + ((a + b) + (c + d))),
                m, x, beside_e, beside_w, from_north(x), from_south(x),
            )

        return (
            tuple(eta),
            tuple(smooth(keep_e, east, from_east(east), west)),
            tuple(smooth(keep_w, west, east, from_west(west))),
            tuple(smooth(keep_n, north, from_east(north), from_west(north))),
        )

    first = tuple(tuple(state[i, v] for v in range(PLANES)) for i in range(4))
    last = lax.fori_loop(0, SUBCYCLES, advance, first, unroll=True)
    return last[0], last[1], last[3]


def store_ocean(last, rows, gather, ocean_o):
    cells = own_cells(last, rows, gather)
    for i, scale in enumerate((1.0, 1.0 / CARRY, 1.0 / CARRY)):
        ocean_o[i] = scale * cells[i]


def kernel(
    state_h, temp_h, land_h, flux_h, w_h, src_h, send_h, mix_h,
    ocean_o, atm_o,
    src_s, send_s, mix_s,
    w_v, wt_v, flux_v, temp_v, land_v, own, fown,
    listing, stage, send1, recv1, send2, recv2,
    packs, fpacks, rows_in, frows_in, sides_in, fsides_in,
    idcol, pick, back, listed, lhs, fscr, rscr, cscr, rows, masks, state, spread, gather,
    load_sem, tile_send, tile_recv, back_send, back_recv,
    halo_send, halo_recv, fhalo_send, fhalo_recv, ready,
):
    comp = lax.axis_index("comp")
    blk = lax.axis_index("blk")
    sub = lax.axis_index("sub")
    row = comp * N_SUB + sub

    def device(dx, dy):
        to_row = lax.rem(row + dy + N_ROW, N_ROW)
        return (to_row // N_SUB, lax.rem(blk + dx + N_BLK, N_BLK), lax.rem(to_row, N_SUB))

    def partner(i):
        away = N_BLK // 2 + (1 - 2 * lax.rem(i + comp, 2)) * (i // 2)
        return lax.rem(blk + away, N_BLK)

    barrier = pltpu.get_barrier_semaphore()

    def greet(i, carry):
        pl.semaphore_signal(barrier, inc=1, device_id=(comp, partner(i), sub), device_id_type=MESH)
        return carry

    lax.fori_loop(1, N_BLK, greet, 0)
    for dy in (1, -1):
        pl.semaphore_signal(barrier, inc=1, device_id=device(0, dy), device_id_type=MESH)

    loads = [
        pltpu.make_async_copy(src, dst, load_sem.at[i])
        for i, (src, dst) in enumerate(
            [
                (mix_h, mix_s), (flux_h, flux_v), (send_h, send_s), (src_h, src_s),
                (state_h, own.at[pl.ds(0, 3)]), (land_h, land_v), (temp_h, temp_v), (w_h, w_v),
            ]
        )
    ]
    for load in loads:
        load.start()

    for load in loads[:3]:
        load.wait()
    stage_tiles(flux_v, send_s, mix_s, listing, stage, send1)

    pl.semaphore_wait(barrier, N_BLK - 1 + 2)
    for dy in (1, -1):
        pl.semaphore_signal(ready, inc=1, device_id=device(0, dy), device_id_type=MESH)

    def send_all(src, dst, send_sem, recv_sem):
        def send(i, carry):
            pltpu.make_async_remote_copy(
                src_ref=src.at[partner(i)], dst_ref=dst.at[blk],
                send_sem=send_sem, recv_sem=recv_sem,
                device_id=(comp, partner(i), sub), device_id_type=MESH,
            ).start()
            return carry

        lax.fori_loop(1, N_BLK, send, 0)

    others = pl.ds(0, N_BLK - 1)

    def all_of(src, dst, sem):
        return pltpu.make_async_copy(src.at[others], dst.at[others], sem)

    send_all(send1, recv1, tile_send, tile_recv)

    def halo_copies(block, pair, rows_to, sides_to, send_sem, recv_sem):
        out = []

        def add(src, dst, dx, dy):
            i = len(out)
            out.append(
                pltpu.make_async_remote_copy(
                    src_ref=src, dst_ref=dst, send_sem=send_sem.at[i], recv_sem=recv_sem.at[i],
                    device_id=device(dx, dy), device_id_type=MESH,
                )
            )

        for slot, dy in ((1, -1), (2, 1), (0, 0)):
            add(pair.at[0], sides_to.at[slot], -1, dy)
            add(pair.at[1], sides_to.at[3 + slot], 1, dy)
        add(block, rows_to.at[0], 0, -1)
        add(block, rows_to.at[1], 0, 1)
        return out

    loads[4].wait()
    loads[5].wait()
    own[3] = land_v[...].astype(f32)
    packs[0], packs[1] = pack_sides([own[i] for i in range(4)])
    recv1[blk] = send1[blk]

    loads[3].wait()
    tables(src_s, send_s, idcol, pick, back, listed)
    column_tables(spread, gather)
    rscr[...] = jnp.zeros_like(rscr)
    loads[6].wait()
    loads[7].wait()
    turn_weights(w_v, wt_v)
    pl.semaphore_wait(ready, 2)
    halo = halo_copies(own, packs, rows_in, sides_in, halo_send, halo_recv)
    for copy in halo:
        copy.start()

    all_of(send1, recv1, tile_recv).wait()
    forcing = remap(pick, recv1, lhs, w_v, fscr)
    fown[0], fown[1] = forcing[0], forcing[1]
    fpacks[0], fpacks[1] = pack_sides(forcing[:2])
    fhalo = halo_copies(fown, fpacks, frows_in, fsides_in, fhalo_send, fhalo_recv)
    for copy in fhalo:
        copy.start()
    remap_back(own[3], temp_v[...], forcing[2] + forcing[3], wt_v, rscr, cscr, back, send2)
    send_all(send2, recv2, back_send, back_recv)
    recv2[blk] = send2[blk]

    for copy in halo:
        copy.wait_recv()
    around = [
        extend(own[i], rows_in[0, i], rows_in[1, i], [sides_in[j] for j in range(6)], i, 4) for i in range(4)
    ]
    start_ocean(around, rows, spread, masks, state)
    for copy in fhalo:
        copy.wait_recv()
    push = [
        extend(fown[i], frows_in[0, i], frows_in[1, i], [fsides_in[j] for j in range(6)], i, 2) for i in range(2)
    ]
    last = subcycles(push, rows, spread, masks, state)

    all_of(send2, recv2, back_recv).wait()
    store_ocean(last, rows, gather, ocean_o)
    gather_back(listed, recv2, atm_o)

    all_of(send1, recv1, tile_send).wait()
    all_of(send2, recv2, back_send).wait()
    for copy in halo + fhalo:
        copy.wait_send()


def shards(ocean_state, sea_temp, land_mask, atm_flux, remap_w, source_tile, send_tiles, flux_mix):
    hbm = pl.BlockSpec(memory_space=pltpu.HBM)
    vmem = pl.BlockSpec(memory_space=pltpu.VMEM)
    message = pltpu.VMEM((N_BLK, CAP, PARTS, TILE), bf16)
    returned = pltpu.VMEM((N_BLK, CAP, 2, TILE), bf16)
    dma = pltpu.SemaphoreType.DMA
    ocean, atm = pl.pallas_call(
        kernel,
        out_shape=(
            jax.ShapeDtypeStruct((3, OY, OX), f32),
            jax.ShapeDtypeStruct((2 * ATILES_DEV, TILE), f32),
        ),
        in_specs=[hbm] * 8,
        out_specs=(vmem, vmem),
        scratch_shapes=[
            pltpu.SMEM((KSRC, 2, OY), i32),
            pltpu.SMEM((1, CAP, 1, N_BLK), i32),
            pltpu.SMEM((3, FIELDS), f32),
            pltpu.VMEM((OY, 2, KSRC, TILE, TILE), bf16),
            pltpu.VMEM((OY // 2, OX, 2 * KSRC * TILE), bf16),
            pltpu.VMEM((FIELDS, ATILES_DEV, TILE), bf16),
            pltpu.VMEM((OY, OX), f32),
            pltpu.VMEM((OY, OX), i32),
            pltpu.VMEM((4, OY, OX), f32),
            pltpu.VMEM((2, OY, OX), f32),
            pltpu.VMEM((N_BLK * MSG, TILE), i32),
            pltpu.VMEM((N_BLK * MSG, 4 * ATILES_DEV), bf16),
            message, message, returned, returned,
            pltpu.VMEM((2, OY, TILE), f32),
            pltpu.VMEM((2, OY, TILE), f32),
            pltpu.VMEM((2, 4, OY, OX), f32),
            pltpu.VMEM((2, 2, OY, OX), f32),
            pltpu.VMEM((6, OY, TILE), f32),
            pltpu.VMEM((6, OY, TILE), f32),
            pltpu.VMEM((ROWS, TILE), i32),
            pltpu.VMEM((ROWS, N_BLK * MSG), bf16),
            pltpu.VMEM((N_BLK * RET, 2 * TILE), bf16),
            pltpu.VMEM((2 * ATILES_DEV, N_BLK * RET), bf16),
            pltpu.VMEM((TILE, KSRC * TILE), bf16),
            pltpu.VMEM((2 * TILE + 8, TILE), f32),
            pltpu.VMEM((8 * OY + 8, TILE), f32),
            pltpu.VMEM((4 * OY, KSRC * TILE), f32),
            pltpu.VMEM((4, COLUMNS * EXT_Y + 8, TILE), f32),
            pltpu.VMEM((7, PLANES, 8, EXT_X), f32),
            pltpu.VMEM((4, PLANES, 8, EXT_X), f32),
            pltpu.VMEM((EXT_X, EXT_X), bf16),
            pltpu.VMEM((EXT_X, OX), bf16),
            dma((8,)),
            dma, dma, dma, dma,
            dma((8,)), dma((8,)), dma((8,)), dma((8,)),
            pltpu.SemaphoreType.REGULAR,
        ],
        compiler_params=pltpu.CompilerParams(
            collective_id=0, has_side_effects=True, vmem_limit_bytes=32 * 1024 * 1024
        ),
    )(
        *(
            pltpu.with_memory_space_constraint(x, pltpu.HBM)
            for x in (
                ocean_state, sea_temp, land_mask,
                jnp.transpose(atm_flux[0], (1, 0, 2)),
                remap_w,
                jnp.transpose(source_tile, (2, 1, 0)),
                jnp.transpose(send_tiles, (0, 3, 1, 2)),
                flux_mix,
            )
        )
    )
    return ocean, atm.reshape(1, ATILES_DEV, 2, TILE)


def solution(mesh):
    placed = (
        P(None, ("comp", "sub"), "blk"),
        P(("comp", "sub"), "blk"),
        P(("comp", "sub"), "blk"),
        P(("comp", "sub"), "blk", None, None),
        P(("comp", "sub"), "blk", None, None, None),
        P(("comp", "sub"), "blk", None),
        P(("comp", "sub"), "blk", None, None),
        P(),
    )
    return jax.shard_map(
        shards,
        mesh=mesh,
        in_specs=placed,
        out_specs=(P(None, ("comp", "sub"), "blk"), P(("comp", "sub"), "blk", None, None)),
        check_vma=False,
    )
```

```python
import functools

import jax
import jax.numpy as jnp
from jax import lax
from jax.experimental import pallas as pl
from jax.experimental.pallas import tpu as pltpu
from jax.sharding import PartitionSpec as P

MESH = pl.DeviceIdType.MESH

SUBCYCLES = 10
FIELDS = 12
TILE = 128
KSRC = 3
CAP = 3
OY = 16
OX = 256
ATILES_DEV = 64
N_BLK = 48
N_ROW = 16
N_SUB = 8

EXT_Y = 40
EXT_X = 384
PLANES = EXT_Y // 8
COLUMNS = EXT_X // TILE

PARTS = 4
MSG = CAP * PARTS
RET = CAP * 2
REFS = KSRC * OY * 2
ROWS = REFS * PARTS

drag_rate = 0.02
gravity_step = 0.6
depth_step = 0.6
force_step = 0.1
spread_rate = 0.1
filter_rate = 0.1

f32 = jnp.float32
bf16 = jnp.bfloat16
i32 = jnp.int32


def iota(shape, dim):
    return lax.broadcasted_iota(i32, shape, dim)


def pack_sides(fields):
    width = TILE // len(fields)
    lane = iota((OY, TILE), 1) // width
    first = last = jnp.zeros((OY, TILE), f32)
    for i, field in enumerate(fields):
        head, tail = field[:, :TILE], field[:, OX - TILE :]
        if i:
            head = pltpu.roll(head, i * width, 1)
        if i + 1 < len(fields):
            tail = pltpu.roll(tail, (i + 1) * width, 1)
        first = jnp.where(lane == i, head, first)
        last = jnp.where(lane == i, tail, last)
    return first, last


def extend(own, north, south, sides, i, count):
    width = TILE // count
    lane = iota((OY, TILE), 1)

    def beside(slot):
        east, west = sides[slot], sides[3 + slot]
        if i:
            east = pltpu.roll(east, TILE - i * width, 1)
        if i + 1 < count:
            west = pltpu.roll(west, TILE - (i + 1) * width, 1)
        return jnp.where(lane < TILE // 2, east, west)

    own = jnp.concatenate([own, beside(0)], axis=1)
    north = jnp.concatenate([north, beside(1)], axis=1)
    south = jnp.concatenate([south, beside(2)], axis=1)
    between = jnp.where(iota((8, EXT_X), 0) < 4, north[8:], south[:8])
    return jnp.concatenate([own, north[:8], between, south[8:]], axis=0)


def stage_tiles(flux_v, send_s, mix_s, listing, stage, send1):
    mixes = []
    for q in range(3):
        total = jnp.zeros((ATILES_DEV, TILE), f32)
        for f in range(FIELDS):
            total = total + mix_s[q, f] * flux_v[f].astype(f32)
        mixes.append(total)
    high = mixes[2].astype(bf16)
    rest = (mixes[2] - high.astype(f32)).astype(bf16)
    mixed = jnp.concatenate([mixes[0].astype(bf16), mixes[1].astype(bf16), high, rest], axis=0)

    upper = iota((8, TILE), 0) < PARTS
    for j in range(0, N_BLK, 2):
        slots = [send_s[0, s, 0, i] for i in (j, j + 1) for s in range(CAP)]
        for i in range(CAP):
            listing[pl.ds(j * MSG + i * 8, 8), :] = jnp.where(upper, slots[2 * i], slots[2 * i + 1])
    wanted = listing[...]
    part = iota((N_BLK * MSG, TILE), 0) % PARTS
    wanted = jnp.where(wanted >= 0, wanted + part * ATILES_DEV, -1)
    for c in range(2):
        stage[:, c * TILE : (c + 1) * TILE] = jnp.where(
            wanted == iota((N_BLK * MSG, TILE), 1) + c * TILE, 1.0, 0.0
        ).astype(bf16)
    rows = jnp.dot(stage[...], mixed, preferred_element_type=f32).astype(bf16)
    send1[...] = rows.reshape(send1.shape)


def tables(src_s, send_s, idcol, pick, back, listed):
    upper = iota((8, TILE), 0) < PARTS
    refs = jnp.full((1, TILE), -1, i32)
    wide = [jnp.full((1, TILE), -1, i32) for _ in range(2)]
    lane1 = iota((1, TILE), 1)
    for k in range(KSRC):
        for y in range(OY):
            both = [src_s[k, n, y] for n in range(2)]
            idcol[pl.ds((k * OY + y) * 8, 8), :] = jnp.where(upper, both[0], both[1])
            for n, value in enumerate(both):
                place = (k * OY + y) * 2 + n
                refs = jnp.where(lane1 == place, value, refs)
                wide[place // 64] = jnp.where(lane1 // 2 == place % 64, value, wide[place // 64])
    ids = idcol[...]
    spot = iota((ROWS, TILE), 0) // PARTS
    part = iota((ROWS, TILE), 0) % PARTS
    at = iota((ROWS, TILE), 1)
    again = jnp.max(jnp.where((ids == refs) & (spot < at), 1, 0), axis=0, keepdims=True)
    owners = ids // ATILES_DEV
    lower = (refs // ATILES_DEV == owners) & (refs < ids) & (again == 0) & (refs >= 0)
    rank = jnp.dot(
        jnp.where(lower, 1.0, 0.0).astype(bf16), jnp.ones((TILE, TILE), bf16), preferred_element_type=f32
    ).astype(i32)
    target = owners * MSG + rank * PARTS + part
    for c in range(0, N_BLK * MSG, TILE):
        width = min(TILE, N_BLK * MSG - c)
        pick[:, c : c + width] = jnp.where(target == at + c, 1.0, 0.0).astype(bf16)[:, :width]
    first = jnp.where(part == 0, rank, 0)
    for c in range(2):
        rank_line = jnp.sum(jnp.where(spot == at // 2 + c * 64, first, 0), axis=0, keepdims=True)
        to = (wide[c] // ATILES_DEV) * RET + rank_line * 2 + lane1 % 2
        to = jnp.where(wide[c] >= 0, to, -1)
        back[:, c * TILE : (c + 1) * TILE] = jnp.where(to == iota((N_BLK * RET, TILE), 0), 1.0, 0.0).astype(bf16)
    slot = [jnp.full((1, TILE), -1, i32) for _ in range(3)]
    for j in range(N_BLK):
        for s in range(CAP):
            place = j * CAP + s
            slot[place // 64] = jnp.where(lane1 // 2 == place % 64, send_s[0, s, 0, j], slot[place // 64])
    for c in range(3):
        width = min(TILE, N_BLK * RET - c * TILE)
        hit = slot[c] * 2 + lane1 % 2 == iota((2 * ATILES_DEV, TILE), 0)
        listed[:, c * TILE : c * TILE + width] = jnp.where(hit, 1.0, 0.0).astype(bf16)[:, :width]


def weights(w_v, y):
    return jnp.concatenate([w_v[y, n].reshape(KSRC * TILE, TILE) for n in range(2)], axis=1)


def turn_weights(w_v, wt_v):
    for y in range(0, OY, 2):
        for i in range(2):
            wt_v[y // 2, :, i * KSRC * TILE : (i + 1) * KSRC * TILE] = weights(w_v, y + i).T


def remap(pick, recv1, lhs, w_v, fscr):
    arrived = recv1[...].reshape(N_BLK * MSG, TILE)
    picked = jnp.dot(pick[...], arrived, preferred_element_type=f32).astype(bf16)
    lhs[...] = jnp.concatenate([picked[k * TILE : (k + 1) * TILE] for k in range(KSRC)], axis=1)
    upper = iota((16, KSRC * TILE), 0) < 8
    for y in range(0, OY, 2):
        both = lhs[pl.ds(y * 8, 16), :]
        halves = [jnp.where(upper, both, 0), jnp.where(upper, 0, both)]
        out = jnp.dot(
            jnp.concatenate(halves, axis=1), jnp.concatenate([weights(w_v, y), weights(w_v, y + 1)], axis=0),
            preferred_element_type=f32,
        )
        for n in range(2):
            fscr[pl.ds(n * TILE + y * 8, 16), :] = out[:, n * TILE : (n + 1) * TILE]
    return [
        jnp.concatenate(
            [fscr[pl.ds(n * (TILE + PARTS) + p, OY, stride=8), :] for n in range(2)], axis=1
        )
        for p in range(PARTS)
    ]


def remap_back(sea, temp, push, wt_v, rscr, cscr, back, send2):
    surface = sea * (temp + push)
    ice = sea * jax.nn.sigmoid(-2.0 * (surface + 1.0))
    for f, field in enumerate((surface, ice)):
        field = field.astype(bf16).astype(f32)
        for n in range(2):
            rscr[pl.ds(n * 4 * OY + 2 * n + f, OY, stride=4), :] = field[:, n * TILE : (n + 1) * TILE]
    returned = jnp.concatenate([rscr[: 4 * OY], rscr[4 * OY : 8 * OY]], axis=1).astype(bf16)
    for y in range(0, OY, 2):
        out = jnp.dot(returned[y // 4 * 16 : y // 4 * 16 + 16], wt_v[y // 2], preferred_element_type=f32)
        for i in range(2):
            start = (y + i) % 4 * 4
            cscr[pl.ds((y + i) * 4, 4), :] = out[start : start + 4, i * KSRC * TILE : (i + 1) * KSRC * TILE]
    terms = jnp.concatenate([cscr[:, k * TILE : (k + 1) * TILE] for k in range(KSRC)], axis=0)
    table = back[:, : 4 * OY * KSRC]
    top = terms.astype(bf16)
    rest = (terms - top.astype(f32)).astype(bf16)
    sums = jnp.dot(table, top, preferred_element_type=f32) + jnp.dot(table, rest, preferred_element_type=f32)
    send2[...] = sums.astype(bf16).reshape(send2.shape)


def gather_back(listed, recv2, atm_o):
    atm_o[...] = jnp.dot(listed[...], recv2[...].reshape(N_BLK * RET, TILE), preferred_element_type=f32)


def reorder(fields, table):
    rows = jnp.concatenate(fields, axis=0)
    top = rows.astype(bf16)
    rest = (rows - top.astype(f32)).astype(bf16)
    out = jnp.dot(
        jnp.concatenate([top, rest], axis=1), jnp.concatenate([table[...]] * 2, axis=0), preferred_element_type=f32
    )
    size = fields[0].shape[0]
    return [out[i * size : (i + 1) * size] for i in range(len(fields))]


def column_tables(spread, gather):
    lane = iota((EXT_X, TILE), 1)
    for t in range(COLUMNS):
        spread[:, t * TILE : (t + 1) * TILE] = jnp.where(
            iota((EXT_X, TILE), 0) == lane * COLUMNS + t, 1.0, 0.0
        ).astype(bf16)
    spot = iota((EXT_X, OX), 0)
    spot = spot % TILE * COLUMNS + spot // TILE
    gather[...] = jnp.where(spot == iota((EXT_X, OX), 1), 1.0, 0.0).astype(bf16)


def interleave(fields, rows, spread):
    out = []
    for i, field in enumerate(reorder(fields, spread)):
        for t in range(COLUMNS):
            rows[i, pl.ds(t * EXT_Y, EXT_Y), :] = field[:, t * TILE : (t + 1) * TILE]
        out.append(
            [
                jnp.concatenate(
                    [rows[i, pl.ds(t * EXT_Y + v, 8, stride=PLANES), :] for t in range(COLUMNS)], axis=1
                )
                for v in range(PLANES)
            ]
        )
    return out


def own_cells(fields, rows, gather):
    out = []
    for i, planes in enumerate(fields):
        for t in range(COLUMNS):
            for v in range(PLANES):
                rows[i, pl.ds(t * EXT_Y + v, 8, stride=PLANES), :] = planes[v][:, t * TILE : (t + 1) * TILE]
        out.append(jnp.concatenate([rows[i, pl.ds(t * EXT_Y, OY), :] for t in range(COLUMNS)], axis=1))
    return reorder(out, gather)


def from_east(planes):
    return [jnp.concatenate([x[:, TILE:], pltpu.roll(x[:, :TILE], TILE - 1, 1)], axis=1) for x in planes]


def from_west(planes):
    return [
        jnp.concatenate([pltpu.roll(x[:, EXT_X - TILE :], 1, 1), x[:, : EXT_X - TILE]], axis=1) for x in planes
    ]


def from_north(planes):
    return planes[1:] + [pltpu.roll(planes[0], 7, 0)]


def from_south(planes):
    return [pltpu.roll(planes[-1], 1, 0)] + planes[:-1]


def each(f, *fields):
    return [f(*planes) for planes in zip(*fields)]


CARRY = depth_step * (1.0 - drag_rate)


def start_ocean(around, rows, spread, masks, state):
    eta, east, north, sea = interleave(around, rows, spread)
    east_open = each(lambda a, b: a * b, sea, from_east(sea))
    north_open = each(lambda a, b: a * b, sea, from_north(sea))
    consts = [
        sea,
        each(lambda m: (gravity_step * depth_step) * m, east_open),
        each(lambda m: (gravity_step * depth_step) * m, north_open),
        each(lambda m: (filter_rate * (1.0 - drag_rate)) * m, east_open),
        each(lambda m: (filter_rate * (1.0 - drag_rate)) * m, north_open),
    ]
    consts += [from_west(consts[1]), from_west(consts[3])]
    east = each(lambda m, w: CARRY * m * w, east_open, east)
    north = each(lambda m, w: CARRY * m * w, north_open, north)
    for ref, fields in ((masks, consts), (state, [eta, east, from_west(east), north])):
        for i, planes in enumerate(fields):
            for v in range(PLANES):
                ref[i, v] = planes[v]


def subcycles(push, rows, spread, masks, state):
    push = interleave(push, rows, spread)
    sea, grad_e, grad_n, keep_e, keep_n, grad_w, keep_w = (
        [masks[i, v] for v in range(PLANES)] for i in range(7)
    )
    push_e, push_n = (
        each(lambda m, f: (force_step / gravity_step) * m * f, grad, field)
        for grad, field in zip((grad_e, grad_n), push)
    )
    push_w = from_west(push_e)
    share = spread_rate / (gravity_step * depth_step)
    centre = (1.0 - 4.0 * filter_rate) / filter_rate

    def advance(_, carried):
        eta, east, west, north = (list(field) for field in carried)
        slope_e = each(lambda m, a, b: m * (a - b), grad_e, from_east(eta), eta)
        slope_w = each(lambda m, a, b: m * (a - b), grad_w, eta, from_west(eta))
        slope_n = each(lambda m, a, b: m * (a - b), grad_n, from_north(eta), eta)
        east = each(lambda w, p, a: w + p - a, east, push_e, slope_e)
        west = each(lambda w, p, a: w + p - a, west, push_w, slope_w)
        north = each(lambda w, p, a: w + p - a, north, push_n, slope_n)
        flow_n = each(lambda w, a: w - share * a, north, slope_n)
        eta = each(
            lambda m, e, a, b, x, y, c, d: m * (e - ((a - b) - share * (x - y)) - (c - d)),
            sea, eta, east, west, slope_e, slope_w, flow_n, from_south(flow_n),
        )

        def smooth(m, x, beside_e, beside_w):
            return each(
                lambda m, x, a, b, c, d: m * (centre * x + ((a + b) + (c + d))),
                m, x, beside_e, beside_w, from_north(x), from_south(x),
            )

        return (
            tuple(eta),
            tuple(smooth(keep_e, east, from_east(east), west)),
            tuple(smooth(keep_w, west, east, from_west(west))),
            tuple(smooth(keep_n, north, from_east(north), from_west(north))),
        )

    first = tuple(tuple(state[i, v] for v in range(PLANES)) for i in range(4))
    last = lax.fori_loop(0, SUBCYCLES, advance, first, unroll=True)
    return last[0], last[1], last[3]


def store_ocean(last, rows, gather, ocean_o):
    cells = own_cells(last, rows, gather)
    for i, scale in enumerate((1.0, 1.0 / CARRY, 1.0 / CARRY)):
        ocean_o[i] = scale * cells[i]


def kernel(
    state_h, temp_h, land_h, flux_h, w_h, src_h, send_h, mix_h,
    ocean_o, atm_o,
    src_s, send_s, mix_s,
    w_v, wt_v, flux_v, temp_v, land_v, own, fown,
    listing, stage, send1, recv1, send2, recv2,
    packs, fpacks, rows_in, frows_in, sides_in, fsides_in,
    idcol, pick, back, listed, lhs, fscr, rscr, cscr, rows, masks, state, spread, gather,
    load_sem, tile_send, tile_recv, back_send, back_recv,
    halo_send, halo_recv, fhalo_send, fhalo_recv, ready,
):
    comp = lax.axis_index("comp")
    blk = lax.axis_index("blk")
    sub = lax.axis_index("sub")
    row = comp * N_SUB + sub

    def device(dx, dy):
        to_row = lax.rem(row + dy + N_ROW, N_ROW)
        return (to_row // N_SUB, lax.rem(blk + dx + N_BLK, N_BLK), lax.rem(to_row, N_SUB))

    def partner(i):
        away = N_BLK // 2 + (1 - 2 * lax.rem(i + comp, 2)) * (i // 2)
        return lax.rem(blk + away, N_BLK)

    barrier = pltpu.get_barrier_semaphore()

    def greet(i, carry):
        pl.semaphore_signal(barrier, inc=1, device_id=(comp, partner(i), sub), device_id_type=MESH)
        return carry

    lax.fori_loop(1, N_BLK, greet, 0)
    for dy in (1, -1):
        pl.semaphore_signal(barrier, inc=1, device_id=device(0, dy), device_id_type=MESH)

    loads = [
        pltpu.make_async_copy(src, dst, load_sem.at[i])
        for i, (src, dst) in enumerate(
            [
                (mix_h, mix_s), (flux_h, flux_v), (send_h, send_s), (src_h, src_s),
                (state_h, own.at[pl.ds(0, 3)]), (land_h, land_v), (temp_h, temp_v), (w_h, w_v),
            ]
        )
    ]
    for load in loads:
        load.start()

    for load in loads[:3]:
        load.wait()
    stage_tiles(flux_v, send_s, mix_s, listing, stage, send1)

    pl.semaphore_wait(barrier, N_BLK - 1 + 2)
    for dy in (1, -1):
        pl.semaphore_signal(ready, inc=1, device_id=device(0, dy), device_id_type=MESH)

    def send_all(src, dst, send_sem, recv_sem):
        def send(i, carry):
            pltpu.make_async_remote_copy(
                src_ref=src.at[partner(i)], dst_ref=dst.at[blk],
                send_sem=send_sem, recv_sem=recv_sem,
                device_id=(comp, partner(i), sub), device_id_type=MESH,
            ).start()
            return carry

        lax.fori_loop(1, N_BLK, send, 0)

    others = pl.ds(0, N_BLK - 1)

    def all_of(src, dst, sem):
        return pltpu.make_async_copy(src.at[others], dst.at[others], sem)

    send_all(send1, recv1, tile_send, tile_recv)

    def halo_copies(block, pair, rows_to, sides_to, send_sem, recv_sem):
        out = []

        def add(src, dst, dx, dy):
            i = len(out)
            out.append(
                pltpu.make_async_remote_copy(
                    src_ref=src, dst_ref=dst, send_sem=send_sem.at[i], recv_sem=recv_sem.at[i],
                    device_id=device(dx, dy), device_id_type=MESH,
                )
            )

        for slot, dy in ((1, -1), (2, 1), (0, 0)):
            add(pair.at[0], sides_to.at[slot], -1, dy)
            add(pair.at[1], sides_to.at[3 + slot], 1, dy)
        add(block, rows_to.at[0], 0, -1)
        add(block, rows_to.at[1], 0, 1)
        return out

    loads[4].wait()
    loads[5].wait()
    own[3] = land_v[...].astype(f32)
    packs[0], packs[1] = pack_sides([own[i] for i in range(4)])
    recv1[blk] = send1[blk]

    loads[3].wait()
    tables(src_s, send_s, idcol, pick, back, listed)
    column_tables(spread, gather)
    rscr[...] = jnp.zeros_like(rscr)
    loads[6].wait()
    loads[7].wait()
    turn_weights(w_v, wt_v)
    pl.semaphore_wait(ready, 2)
    halo = halo_copies(own, packs, rows_in, sides_in, halo_send, halo_recv)
    for copy in halo:
        copy.start()

    all_of(send1, recv1, tile_recv).wait()
    forcing = remap(pick, recv1, lhs, w_v, fscr)
    fown[0], fown[1] = forcing[0], forcing[1]
    fpacks[0], fpacks[1] = pack_sides(forcing[:2])
    fhalo = halo_copies(fown, fpacks, frows_in, fsides_in, fhalo_send, fhalo_recv)
    for copy in fhalo:
        copy.start()
    remap_back(own[3], temp_v[...], forcing[2] + forcing[3], wt_v, rscr, cscr, back, send2)
    send_all(send2, recv2, back_send, back_recv)
    recv2[blk] = send2[blk]

    for copy in halo:
        copy.wait_recv()
    around = [
        extend(own[i], rows_in[0, i], rows_in[1, i], [sides_in[j] for j in range(6)], i, 4) for i in range(4)
    ]
    start_ocean(around, rows, spread, masks, state)
    all_of(send2, recv2, back_recv).wait()
    gather_back(listed, recv2, atm_o)
    for copy in fhalo:
        copy.wait_recv()
    push = [
        extend(fown[i], frows_in[0, i], frows_in[1, i], [fsides_in[j] for j in range(6)], i, 2) for i in range(2)
    ]
    last = subcycles(push, rows, spread, masks, state)

    store_ocean(last, rows, gather, ocean_o)

    all_of(send1, recv1, tile_send).wait()
    all_of(send2, recv2, back_send).wait()
    for copy in halo + fhalo:
        copy.wait_send()


def shards(ocean_state, sea_temp, land_mask, atm_flux, remap_w, source_tile, send_tiles, flux_mix):
    hbm = pl.BlockSpec(memory_space=pltpu.HBM)
    vmem = pl.BlockSpec(memory_space=pltpu.VMEM)
    message = pltpu.VMEM((N_BLK, CAP, PARTS, TILE), bf16)
    returned = pltpu.VMEM((N_BLK, CAP, 2, TILE), bf16)
    dma = pltpu.SemaphoreType.DMA
    ocean, atm = pl.pallas_call(
        kernel,
        out_shape=(
            jax.ShapeDtypeStruct((3, OY, OX), f32),
            jax.ShapeDtypeStruct((2 * ATILES_DEV, TILE), f32),
        ),
        in_specs=[hbm] * 8,
        out_specs=(vmem, vmem),
        scratch_shapes=[
            pltpu.SMEM((KSRC, 2, OY), i32),
            pltpu.SMEM((1, CAP, 1, N_BLK), i32),
            pltpu.SMEM((3, FIELDS), f32),
            pltpu.VMEM((OY, 2, KSRC, TILE, TILE), bf16),
            pltpu.VMEM((OY // 2, OX, 2 * KSRC * TILE), bf16),
            pltpu.VMEM((FIELDS, ATILES_DEV, TILE), bf16),
            pltpu.VMEM((OY, OX), f32),
            pltpu.VMEM((OY, OX), i32),
            pltpu.VMEM((4, OY, OX), f32),
            pltpu.VMEM((2, OY, OX), f32),
            pltpu.VMEM((N_BLK * MSG, TILE), i32),
            pltpu.VMEM((N_BLK * MSG, 4 * ATILES_DEV), bf16),
            message, message, returned, returned,
            pltpu.VMEM((2, OY, TILE), f32),
            pltpu.VMEM((2, OY, TILE), f32),
            pltpu.VMEM((2, 4, OY, OX), f32),
            pltpu.VMEM((2, 2, OY, OX), f32),
            pltpu.VMEM((6, OY, TILE), f32),
            pltpu.VMEM((6, OY, TILE), f32),
            pltpu.VMEM((ROWS, TILE), i32),
            pltpu.VMEM((ROWS, N_BLK * MSG), bf16),
            pltpu.VMEM((N_BLK * RET, 2 * TILE), bf16),
            pltpu.VMEM((2 * ATILES_DEV, N_BLK * RET), bf16),
            pltpu.VMEM((TILE, KSRC * TILE), bf16),
            pltpu.VMEM((2 * TILE + 8, TILE), f32),
            pltpu.VMEM((8 * OY + 8, TILE), f32),
            pltpu.VMEM((4 * OY, KSRC * TILE), f32),
            pltpu.VMEM((4, COLUMNS * EXT_Y + 8, TILE), f32),
            pltpu.VMEM((7, PLANES, 8, EXT_X), f32),
            pltpu.VMEM((4, PLANES, 8, EXT_X), f32),
            pltpu.VMEM((EXT_X, EXT_X), bf16),
            pltpu.VMEM((EXT_X, OX), bf16),
            dma((8,)),
            dma, dma, dma, dma,
            dma((8,)), dma((8,)), dma((8,)), dma((8,)),
            pltpu.SemaphoreType.REGULAR,
        ],
        compiler_params=pltpu.CompilerParams(
            collective_id=0, has_side_effects=True, vmem_limit_bytes=32 * 1024 * 1024
        ),
    )(
        *(
            pltpu.with_memory_space_constraint(x, pltpu.HBM)
            for x in (
                ocean_state, sea_temp, land_mask,
                jnp.transpose(atm_flux[0], (1, 0, 2)),
                remap_w,
                jnp.transpose(source_tile, (2, 1, 0)),
                jnp.transpose(send_tiles, (0, 3, 1, 2)),
                flux_mix,
            )
        )
    )
    return ocean, atm.reshape(1, ATILES_DEV, 2, TILE)


def solution(mesh):
    placed = (
        P(None, ("comp", "sub"), "blk"),
        P(("comp", "sub"), "blk"),
        P(("comp", "sub"), "blk"),
        P(("comp", "sub"), "blk", None, None),
        P(("comp", "sub"), "blk", None, None, None),
        P(("comp", "sub"), "blk", None),
        P(("comp", "sub"), "blk", None, None),
        P(),
    )
    return jax.shard_map(
        shards,
        mesh=mesh,
        in_specs=placed,
        out_specs=(P(None, ("comp", "sub"), "blk"), P(("comp", "sub"), "blk", None, None)),
        check_vma=False,
    )
```
